128 devices in a mesh: scene: 32 (over x, y, core), grp: 4 (over z).
Axes of the slice: x: 4, y: 4, z: 4, core: 2. Of those that a mesh axis runs over, the one named last changes fastest.
Arguments:
- windows: bfloat16 [128, 4, 512, 512], P(('scene', 'grp')), may hold values from -6 to 6
- counts: int32 [128], P(('scene', 'grp')), may hold values from 1 to 4, as said below
- intersection_pairs: int32 [128, 4], P(('scene', 'grp')), may hold values from 0 to 127, as said below
Outputs:
- surfaces: float32 [128, 4, 512, 512], P(('scene', 'grp'))
The draws below stay inside these ranges and needn't reach their ends.
Inputs may be any that keep to these rules, and one draw needn't show every extreme that they name: The counts of all scenes sum to 256. `intersection_pairs`: columns are scene, window, scene, window. Every slot (s, w) with w < counts[s] is named exactly once in the whole list; no other slot is named.
All inputs are finite; a program needn't handle non-finite values.
Results may differ from the reference program's by a relative error of at most 0.009.
Values may be sent and summed in bfloat16 or wider, within the bound.
No kernel may reach another device: no remote copies, remote signals or barrier semaphores. Data moves between devices by JAX's collectives and lax.ppermute only.
A program may use at most 128 MiB of HBM per device.

```python
import math
import jax
import jax.numpy as jnp
from jax import lax

W = 512
WMAX = 4
SCENES = 128
SLOTS = 512
PAIRS = 128


def strip_counts(key):
    ordering = jax.random.permutation(key, SCENES)
    pattern = jnp.array([WMAX, 1, WMAX // 2 - 1, WMAX // 2], dtype=jnp.int32)
    return pattern[ordering % 4]


def draw_counts(key, part):
    shared = strip_counts(key)
    return shared.astype(jnp.int32)


def draw_intersection_pairs(key, part):
    shared = strip_counts(key)
    key = jax.random.fold_in(key, 7)
    window_index = jnp.arange(WMAX, dtype=jnp.int32)
    in_use = (window_index[None, :] < shared[:, None]).reshape(-1)
    ordering = jnp.argsort(jnp.where(in_use, 0, 1).astype(jnp.int32), stable=True).astype(jnp.int32)
    used_slots = ordering[:2 * PAIRS]
    shuffle = jax.random.permutation(key, PAIRS)
    first_slot = used_slots[:PAIRS]
    second_slot = used_slots[PAIRS:][shuffle]
    return jnp.stack([first_slot // WMAX, first_slot % WMAX, second_slot // WMAX, second_slot % WMAX], axis=1).astype(jnp.int32)


def block_scale(stream_key, extent, pieces, least, largest):
    loudness, own = 1.0, jax.random.fold_in(stream_key, 6)
    for position, shards_of in pieces:
        steps = jnp.exp(jax.random.uniform(jax.random.fold_in(own, position), (shards_of,), jnp.float32, least / len(pieces), largest / len(pieces)))
        loudness = loudness * jnp.repeat(steps, extent[position] // shards_of).reshape([-1 if axis == position else 1 for axis in range(len(extent))])
    return loudness


def bell_draw(rng, dims, scale, most, cuts=(), kind=jnp.bfloat16):
    entries = scale * jax.random.normal(rng, dims, jnp.float32)
    if cuts:
        entries = entries * block_scale(rng, dims, cuts, -0.22, 0.18)
    return jnp.clip(entries, -most, most).astype(kind)


def setup_inputs(seed: int = 0) -> dict:
    key_of = jax.random.split(jax.random.key(seed), 4)
    return {
        "windows": bell_draw(key_of[0], (SCENES, WMAX, W, W), 1.0, 6.0, ((0, 128),)),
        "counts": draw_counts(jax.random.fold_in(key_of[3], 71), 0),
        "intersection_pairs": draw_intersection_pairs(jax.random.fold_in(key_of[3], 71), 0),
    }


def dft_tables(length):
    indices = jnp.arange(length, dtype=jnp.int32)
    product = indices[:, None] * indices[None, :] % length
    angles = product.astype(jnp.float32) * (2.0 * math.pi / length)
    return (jnp.cos(angles).astype(jnp.bfloat16), jnp.sin(angles).astype(jnp.bfloat16))

def normalize(window):
    values = window.astype(jnp.float32)
    centered = values - lax.optimization_barrier(jnp.mean(values, axis=(-2, -1), keepdims=True))
    spread = lax.rsqrt(lax.optimization_barrier(jnp.mean(centered * centered, axis=(-2, -1), keepdims=True)) + 1e-05)
    return (centered * spread).astype(jnp.bfloat16)

def spectrum(window, cos_table, sin_table):
    normed = normalize(window)
    row_real = jnp.dot(normed, cos_table, preferred_element_type=jnp.float32).astype(jnp.bfloat16)
    row_imag = (-jnp.dot(normed, sin_table, preferred_element_type=jnp.float32)).astype(jnp.bfloat16)
    spec_real = jnp.dot(cos_table, row_real, preferred_element_type=jnp.float32) + jnp.dot(sin_table, row_imag, preferred_element_type=jnp.float32)
    spec_imag = jnp.dot(cos_table, row_imag, preferred_element_type=jnp.float32) - jnp.dot(sin_table, row_real, preferred_element_type=jnp.float32)
    return (spec_real, spec_imag)

def surface_of(own_real, own_imag, other_real, other_imag, cos_table, sin_table):
    cross_real = (own_real * other_real + own_imag * other_imag).astype(jnp.bfloat16)
    cross_imag = (own_imag * other_real - own_real * other_imag).astype(jnp.bfloat16)
    scale_back = 1.0 / (W * W)
    back_real = ((jnp.dot(cos_table, cross_real, preferred_element_type=jnp.float32) - jnp.dot(sin_table, cross_imag, preferred_element_type=jnp.float32)) * scale_back).astype(jnp.bfloat16)
    back_imag = ((jnp.dot(cos_table, cross_imag, preferred_element_type=jnp.float32) + jnp.dot(sin_table, cross_real, preferred_element_type=jnp.float32)) * scale_back).astype(jnp.bfloat16)
    return (jnp.dot(back_real, cos_table, preferred_element_type=jnp.float32) - jnp.dot(back_imag, sin_table, preferred_element_type=jnp.float32)) * (1.0 / W)

def reference(windows, counts, intersection_pairs):
    cos_table, sin_table = dft_tables(W)
    flat = windows.reshape(SLOTS, W, W)
    first_slot = (intersection_pairs[:, 0] * WMAX + intersection_pairs[:, 1]).astype(jnp.int32)
    second_slot = (intersection_pairs[:, 2] * WMAX + intersection_pairs[:, 3]).astype(jnp.int32)

    def one_pair(slot_pair):
        first_real, first_imag = spectrum(flat[slot_pair[0]], cos_table, sin_table)
        second_real, second_imag = spectrum(flat[slot_pair[1]], cos_table, sin_table)
        surface_first = surface_of(first_real, first_imag, second_real, second_imag, cos_table, sin_table)
        surface_second = surface_of(second_real, second_imag, first_real, first_imag, cos_table, sin_table)
        return (surface_first, surface_second)
    surface_first, surface_second = lax.map(one_pair, (first_slot, second_slot))
    surfaces = jnp.zeros((SLOTS, W, W), jnp.float32)
    surfaces = surfaces.at[first_slot].set(surface_first).at[second_slot].set(surface_second)
    window_index = jnp.arange(WMAX, dtype=jnp.int32)
    keep_mask = (window_index[None, :] < counts[:, None]).astype(jnp.float32).reshape(SLOTS)
    surfaces = surfaces * keep_mask[:, None, None]
    return surfaces.reshape(SCENES, WMAX, W, W)
```

```python
import functools

import jax
import jax.numpy as jnp
import numpy as np
from jax import lax
from jax.experimental import pallas as pl
from jax.experimental.pallas import tpu as pltpu
from jax.sharding import PartitionSpec as P

AXES = ("scene", "grp")
LENGTH = 512
SLOTS_HELD = 4
LANES = 128
LANE_BLOCKS = LENGTH // LANES
BF16 = jnp.bfloat16
F32 = jnp.float32


def packed_tables(devices):
    places = np.arange(LENGTH)
    packed = LENGTH // devices
    forward = np.zeros((devices, packed, LENGTH))
    backward = np.zeros((devices, packed, LENGTH))
    for dev in range(devices):
        for part in range(packed):
            freq = dev * (packed // 2) + part // 2
            angle = 2.0 * np.pi * ((freq * places) % LENGTH) / LENGTH
            if part % 2 == 0:
                forward[dev, part] = np.cos(angle)
                backward[dev, part] = np.cos(angle) * (1.0 if freq == 0 else 2.0)
            elif freq == 0:
                forward[dev, part] = 1.0 - 2.0 * (places % 2)
                backward[dev, part] = 1.0 - 2.0 * (places % 2)
            else:
                forward[dev, part] = -np.sin(angle)
                backward[dev, part] = -2.0 * np.sin(angle)
    forward = forward.reshape(2, devices // 2, packed, LENGTH).transpose(1, 0, 2, 3)
    forward = forward.reshape(LENGTH, LENGTH).astype(jnp.bfloat16)
    backward = backward.reshape(LENGTH, LENGTH).T / LENGTH
    product = places[:, None] * places[None, :] % LENGTH
    angle = 2.0 * np.pi * product / LENGTH
    both = np.concatenate([np.cos(angle), np.sin(angle)], axis=1)
    row_sum = forward.astype(np.float64).sum(axis=1)
    row_sum = np.broadcast_to(row_sum[:, None], (LENGTH, LANES)).astype(np.float32)
    return forward, row_sum, both.astype(jnp.bfloat16), backward.astype(jnp.bfloat16)


def split_rows(value, rows):
    return value.reshape(value.shape[0] // rows, rows, value.shape[1])


def forward_kernel(pair_ref, x_ref, table_ref, sum_ref, out_ref):
    half = pl.program_id(0)
    groups = LENGTH // 8
    entries = float(LENGTH * LENGTH)
    spectra = []
    for j in range(2):
        values = x_ref[j].astype(F32)
        mean = jnp.sum(values) / entries
        centered = values - mean
        scale = lax.rsqrt(jnp.sum(centered * centered) / entries + 1e-05)
        product = jnp.dot(table_ref[...], x_ref[j], preferred_element_type=F32)
        shift = jnp.concatenate([sum_ref[...] * mean] * LANE_BLOCKS, axis=1)
        spectra.append(split_rows((product - shift) * scale, 8))
    first, second = spectra
    upper = lax.broadcasted_iota(jnp.int32, first.shape, 1) < 4
    low = jnp.where(upper, first, pltpu.roll(second, 4, 1)).astype(BF16)
    high = jnp.where(upper, pltpu.roll(first, 4, 1), second).astype(BF16)
    for step in range(2):
        @pl.when(half == step)
        def _():
            for block in range(LANE_BLOCKS):
                rows = pl.ds(block * 16 + step * 8, 8)
                lanes = slice(block * LANES, (block + 1) * LANES)
                out_ref[pl.ds(0, groups), rows, :] = low[:, :, lanes]
                out_ref[pl.ds(groups, groups), rows, :] = high[:, :, lanes]
    row = lax.broadcasted_iota(jnp.int32, (8, LANES), 0)
    named = jnp.zeros((8, LANES), F32)
    for column in range(4):
        named = jnp.where(row == column, pair_ref[0, column].astype(F32), named)
    out_ref[:, pl.ds(LANE_BLOCKS * 16, 8), :] = jnp.broadcast_to(
        named[None], (2 * groups, 8, LANES)
    ).astype(BF16)


def cross_kernel(first_ref, m_ref, both_ref, out_ref, rows_ref, names_ref):
    devices = m_ref.shape[0]
    slots = devices * SLOTS_HELD
    pairs = devices
    is_first = first_ref[0] == 0
    table = both_ref[...]

    names_ref[...] = m_ref[:, pl.ds(LANE_BLOCKS * 16, 8), :].astype(F32).reshape(devices * 8, LANES)
    named = [names_ref[pl.ds(column, devices, stride=8), :] for column in range(4)]
    slot_rows = [
        (named[2 * side] * SLOTS_HELD + named[2 * side + 1]).astype(jnp.int32) for side in range(2)
    ]
    same = lax.broadcasted_iota(jnp.int32, (pairs, LANES), 0) == lax.broadcasted_iota(
        jnp.int32, (pairs, LANES), 1
    )
    slot_lanes = [
        jnp.sum(jnp.where(same, slot_rows[side], 0), axis=0, keepdims=True) for side in range(2)
    ]
    wanted = jnp.concatenate(
        [jnp.concatenate([slot_rows[side]] * (slots // LANES), axis=1) for side in range(2)], axis=0
    )
    pick = (wanted == lax.broadcasted_iota(jnp.int32, (2 * pairs, slots), 1)).astype(F32).astype(BF16)

    for block in range(LANE_BLOCKS):
        rows_ref[block] = m_ref[:, pl.ds(block * 16, 16), :].astype(F32).reshape(devices * 16, LANES)

    def part_rows(part):
        return jnp.concatenate(
            [rows_ref[block, pl.ds(part, slots, stride=4), :] for block in range(LANE_BLOCKS)], axis=1
        ).astype(BF16)

    inverse = []
    for freq in range(2):
        products = []
        for part in (2 * freq, 2 * freq + 1):
            picked = jnp.dot(pick, part_rows(part), preferred_element_type=F32).astype(BF16)
            products.append(jnp.dot(picked, table, preferred_element_type=F32))
        re_cos, re_sin = products[0][:, :LENGTH], products[0][:, LENGTH:]
        im_cos, im_sin = products[1][:, :LENGTH], products[1][:, LENGTH:]

        def cross(real, imag):
            own_real, other_real = real[:pairs], real[pairs:]
            own_imag, other_imag = imag[:pairs], imag[pairs:]
            return (
                own_real * other_real + own_imag * other_imag,
                own_imag * other_real - own_real * other_imag,
            )

        cross_real, cross_imag = cross(re_cos + im_sin, im_cos - re_sin)
        if freq == 0:
            low_real, low_imag = cross(re_cos, -re_sin)
            top_real, top_imag = cross(im_cos, -im_sin)
            cross_real = jnp.where(is_first, low_real - top_imag, cross_real)
            cross_imag = jnp.where(is_first, low_imag + top_real, cross_imag)
        crossed = jnp.concatenate([cross_real, cross_imag], axis=0).astype(BF16)
        back = jnp.dot(crossed, table, preferred_element_type=F32) * (1.0 / (LENGTH * LENGTH))
        real_cos, real_sin = back[:pairs, :LENGTH], back[:pairs, LENGTH:]
        imag_cos, imag_sin = back[pairs:, :LENGTH], back[pairs:, LENGTH:]
        own_imag = imag_cos + real_sin
        other_imag = real_sin - imag_cos
        if freq == 0:
            other_imag = jnp.where(is_first, imag_cos - real_sin, other_imag)
        inverse.append(
            jnp.concatenate(
                [real_cos - imag_sin, real_cos + imag_sin, own_imag, other_imag], axis=0
            ).astype(BF16)
        )

    row = lax.broadcasted_iota(jnp.int32, (devices * 8, 4 * pairs), 0)
    row_code = row // 8 * SLOTS_HELD + row % SLOTS_HELD + row // SLOTS_HELD % 2 * slots
    lane_code = jnp.concatenate(
        [slot_lanes[0], slot_lanes[1], slot_lanes[0] + slots, slot_lanes[1] + slots], axis=1
    )
    place = (row_code == lane_code).astype(F32).astype(BF16)
    placed = [
        split_rows(jnp.dot(place, inverse[freq], preferred_element_type=F32), 8)
        for freq in range(2)
    ]
    placed = jnp.concatenate(placed, axis=1).astype(BF16)
    for block in range(LANE_BLOCKS):
        out_ref[:, pl.ds(block * 16, 16), :] = placed[:, :, block * LANES : (block + 1) * LANES]


def surface_kernel(count_ref, m_ref, table_ref, out_ref, rows_ref):
    devices = m_ref.shape[0]
    slot = pl.program_id(0)

    @pl.when(slot == 0)
    def _():
        for block in range(LANE_BLOCKS):
            rows_ref[block] = (
                m_ref[:, pl.ds(block * 16, 16), :].astype(F32).reshape(devices * 16, LANES)
            )

    for step in range(SLOTS_HELD):
        @pl.when(slot == step)
        def _():
            rows = jnp.concatenate(
                [
                    rows_ref[block, pl.ds(step, LENGTH, stride=SLOTS_HELD), :]
                    for block in range(LANE_BLOCKS)
                ],
                axis=1,
            ).astype(BF16)
            keep = (step < count_ref[0]).astype(F32)
            out_ref[0, 0] = jnp.dot(table_ref[...], rows, preferred_element_type=F32) * keep


def per_device(windows, counts, intersection_pairs):
    devices = lax.axis_size(AXES)
    position = lax.axis_index(AXES).astype(jnp.int32).reshape(1)
    forward, row_sum, both, backward = packed_tables(devices)
    smem = pl.BlockSpec(memory_space=pltpu.SMEM)
    whole = lambda *shape: pl.BlockSpec(shape, lambda *_: (0,) * len(shape))
    params = lambda: pltpu.CompilerParams(vmem_limit_bytes=56 << 20)
    chunk_rows = LANE_BLOCKS * 16

    sent = pl.pallas_call(
        forward_kernel,
        grid=(2,),
        in_specs=[
            smem,
            pl.BlockSpec((2, LENGTH, LENGTH), lambda h: (h, 0, 0)),
            whole(LENGTH, LENGTH),
            whole(LENGTH, LANES),
        ],
        out_specs=whole(devices, chunk_rows + 8, LANES),
        out_shape=jax.ShapeDtypeStruct((devices, chunk_rows + 8, LANES), BF16),
        compiler_params=params(),
        name="forward_rows",
    )(intersection_pairs, windows[0], jnp.asarray(forward), jnp.asarray(row_sum))
    moved = lax.all_to_all(sent, AXES, 0, 0, tiled=True)
    crossed = pl.pallas_call(
        cross_kernel,
        grid=(1,),
        in_specs=[
            smem,
            whole(devices, chunk_rows + 8, LANES),
            whole(LENGTH, 2 * LENGTH),
        ],
        out_specs=whole(devices, chunk_rows, LANES),
        out_shape=jax.ShapeDtypeStruct((devices, chunk_rows, LANES), BF16),
        scratch_shapes=[
            pltpu.VMEM((LANE_BLOCKS, devices * 16, LANES), F32),
            pltpu.VMEM((devices * 8, LANES), F32),
        ],
        compiler_params=params(),
        name="cross_columns",
    )(position, moved, jnp.asarray(both))
    returned = lax.all_to_all(crossed, AXES, 0, 0, tiled=True)
    return pl.pallas_call(
        surface_kernel,
        grid=(SLOTS_HELD,),
        in_specs=[
            smem,
            whole(devices, chunk_rows, LANES),
            whole(LENGTH, LENGTH),
        ],
        out_specs=pl.BlockSpec((1, 1, LENGTH, LENGTH), lambda s: (0, s, 0, 0)),
        out_shape=jax.ShapeDtypeStruct((1, SLOTS_HELD, LENGTH, LENGTH), F32),
        scratch_shapes=[pltpu.VMEM((LANE_BLOCKS, devices * 16, LANES), F32)],
        compiler_params=params(),
        name="surfaces",
    )(counts, returned, jnp.asarray(backward))


def solution(mesh):
    in_specs = (P(AXES, None, None, None), P(AXES), P(AXES, None))
    out_specs = P(AXES, None, None, None)
    return jax.shard_map(
        per_device, mesh=mesh, in_specs=in_specs, out_specs=out_specs, check_vma=False
    )
```

```python
import jax
import jax.numpy as jnp
import numpy as np
from jax import lax
from jax.experimental import pallas as pl
from jax.experimental.pallas import tpu as pltpu
from jax.sharding import PartitionSpec as P

AXES = ("scene", "grp")
LENGTH = 512
HALF = LENGTH // 2
SLOTS_HELD = 4
LANES = 128
LANE_BLOCKS = LENGTH // LANES
CHUNK = LANE_BLOCKS * 16
BF16 = jnp.bfloat16
F32 = jnp.float32


def packed_tables(devices):
    places = np.arange(LENGTH)
    packed = LENGTH // devices
    forward = np.zeros((devices, packed, LENGTH))
    backward = np.zeros((devices, packed, LENGTH))
    for dev in range(devices):
        for part in range(packed):
            freq = dev * (packed // 2) + part // 2
            angle = 2.0 * np.pi * ((freq * places) % LENGTH) / LENGTH
            if part % 2 == 0:
                forward[dev, part] = np.cos(angle)
                backward[dev, part] = np.cos(angle) * (1.0 if freq == 0 else 2.0)
            elif freq == 0:
                forward[dev, part] = 1.0 - 2.0 * (places % 2)
                backward[dev, part] = 1.0 - 2.0 * (places % 2)
            else:
                forward[dev, part] = -np.sin(angle)
                backward[dev, part] = -2.0 * np.sin(angle)
    forward = forward.reshape(2, devices // 2, packed, LENGTH).transpose(1, 0, 2, 3)
    forward = forward.reshape(LENGTH, LENGTH)
    backward = backward.reshape(LENGTH, LENGTH).T / LENGTH
    product = places[:, None] * places[None, :] % LENGTH
    cosine = np.cos(2.0 * np.pi * product / LENGTH)
    sine = np.sin(2.0 * np.pi * product / LENGTH)
    packed_sine = np.concatenate([cosine[:, HALF : HALF + 1], sine[:, 1:HALF]], axis=1)
    columns = np.concatenate([cosine[:, :HALF], packed_sine], axis=1)
    columns_back = np.stack([cosine[:HALF], sine[:HALF]])
    columns_back[1, 0] = 0.0
    order = np.arange(4 * 64)
    gather = np.zeros((4 * 64, 4 * 64))
    gather[order, order % 64 * 4 + order // 64] = 1.0
    tables = (forward, backward, columns, columns_back, gather)
    return tuple(jnp.asarray(table.astype(jnp.bfloat16)) for table in tables)


def split_rows(value, rows):
    return value.reshape(value.shape[0] // rows, rows, value.shape[1])


def wide(value):
    return jnp.concatenate([value] * LANE_BLOCKS, axis=1)


def total(value):
    return jnp.sum(jnp.sum(value, axis=0, keepdims=True), axis=1, keepdims=True)


def moments(x_ref, slot):
    rows = 16
    steps = LENGTH // rows
    entries = float(LENGTH * LENGTH)
    base = x_ref[slot, 0:rows, :].astype(F32)
    first = jnp.zeros_like(base)
    second = jnp.zeros_like(base)
    for step in range(1, steps):
        diff = x_ref[slot, step * rows : (step + 1) * rows, :].astype(F32) - base
        first = first + diff
        second = second + diff * diff
    local = base + first * (1.0 / steps)
    mean = total(local) * (steps / entries)
    off = local - mean
    spread = total(second - first * first * (1.0 / steps) + off * off * float(steps))
    return mean, lax.rsqrt(spread * (1.0 / entries) + 1e-05)


def forward_kernel(
    pair_hbm, x_hbm, table_hbm, out_hbm, pair_ref, x_ref, table_ref, out_ref, in_sem, late_sem, out_sem
):
    devices = out_ref.shape[0]
    groups = devices // 2
    blocks = 4
    reads = [pltpu.make_async_copy(x_hbm.at[s], x_ref.at[s], in_sem.at[s]) for s in range(SLOTS_HELD)]
    table_read = pltpu.make_async_copy(table_hbm, table_ref, late_sem.at[0])
    pair_read = pltpu.make_async_copy(pair_hbm, pair_ref, late_sem.at[1])
    reads[0].start()
    table_read.start()
    for read in reads[1:]:
        read.start()
    pair_read.start()
    ones = jnp.ones((LENGTH, LANES), BF16)
    spectra = []
    writes = []
    for s in range(SLOTS_HELD):
        reads[s].wait()
        mean, scale = moments(x_ref, s)
        if s == 0:
            table_read.wait()
            row_sum = jnp.dot(table_ref[...], ones, preferred_element_type=F32)
        product = jnp.dot(table_ref[...], x_ref[s], preferred_element_type=F32)
        spectra.append(split_rows(product * scale - wide(row_sum * (mean * scale)), 8))
        if s % 2 == 0:
            continue
        if s == 1:
            pair_read.wait()
            row = lax.broadcasted_iota(jnp.int32, (8, LANES), 0)
            named = jnp.zeros((8, LANES), F32)
            for column in range(4):
                named = jnp.where(row == column, pair_ref[0, column].astype(F32), named)
            out_ref[:, pl.ds(CHUNK, 8), :] = jnp.broadcast_to(
                named[None], (devices, 8, LANES)
            ).astype(BF16)
        count = groups // blocks
        for block in range(blocks):
            one, two = (part[block * count : (block + 1) * count] for part in spectra[s - 1 :])
            upper = lax.broadcasted_iota(jnp.int32, one.shape, 1) < 4
            low = jnp.where(upper, one, pltpu.roll(two, 4, 1)).astype(BF16)
            high = jnp.where(upper, pltpu.roll(one, 4, 1), two).astype(BF16)
            for side, filled in enumerate((low, high)):
                place = pl.ds(side * groups + block * count, count)
                for lane in range(LANE_BLOCKS):
                    start = lane * 16 + s // 2 * 8
                    out_ref[place, start : start + 8, :] = filled[
                        :, :, lane * LANES : (lane + 1) * LANES
                    ]
                if s == SLOTS_HELD - 1:
                    write = pltpu.make_async_copy(
                        out_ref.at[place], out_hbm.at[place], out_sem.at[2 * block + side]
                    )
                    write.start()
                    writes.append(write)
    for write in writes:
        write.wait()


def take_parts(m_ref, gather, parts_ref):
    for block in range(m_ref.shape[0] // 16):
        rows = jnp.concatenate(
            [
                m_ref[block * 16 : (block + 1) * 16, lane * 16 : (lane + 1) * 16, :].reshape(256, LANES)
                for lane in range(LANE_BLOCKS)
            ],
            axis=1,
        )
        taken = jnp.dot(gather, rows, preferred_element_type=F32).astype(BF16)
        for part in range(4):
            parts_ref[part, block * 64 : (block + 1) * 64, :] = taken[part * 64 : (part + 1) * 64]


def cross(real, imag):
    pairs = real.shape[0] // 2
    own_real, other_real = real[:pairs], real[pairs:]
    own_imag, other_imag = imag[:pairs], imag[pairs:]
    return (
        own_real * other_real + own_imag * other_imag,
        own_imag * other_real - own_real * other_imag,
    )


def cross_kernel(
    first_ref, m_ref, columns_ref, back_ref, gather_ref, out_hbm, parts_ref, names_ref, out_ref, out_sem
):
    devices = m_ref.shape[0]
    slots = devices * SLOTS_HELD
    pairs = devices
    is_first = first_ref[0] == 0

    names_ref[...] = m_ref[:, pl.ds(CHUNK, 8), :].astype(F32).reshape(devices * 8, LANES)
    named = [names_ref[pl.ds(column, devices, stride=8), :] for column in range(4)]
    slot_rows = [
        (named[2 * side] * SLOTS_HELD + named[2 * side + 1]).astype(jnp.int32) for side in range(2)
    ]
    same = lax.broadcasted_iota(jnp.int32, (pairs, LANES), 0) == lax.broadcasted_iota(
        jnp.int32, (pairs, LANES), 1
    )
    slot_lanes = [
        jnp.sum(jnp.where(same, slot_rows[side], 0), axis=0, keepdims=True) for side in range(2)
    ]
    wanted = jnp.concatenate([wide(slot_rows[side]) for side in range(2)], axis=0)
    pick = (wanted == lax.broadcasted_iota(jnp.int32, (2 * pairs, slots), 1)).astype(F32).astype(BF16)
    row = lax.broadcasted_iota(jnp.int32, (devices * 8, 4 * pairs), 0)
    row_code = (row >> 3) * SLOTS_HELD + (row & 3) + ((row >> 2) & 1) * slots
    lane_code = jnp.concatenate(
        [slot_lanes[0], slot_lanes[1], slot_lanes[0] + slots, slot_lanes[1] + slots], axis=1
    )
    place = (row_code == lane_code).astype(F32).astype(BF16)

    take_parts(m_ref, gather_ref[...], parts_ref)

    zero = lax.broadcasted_iota(jnp.int32, (2 * pairs, HALF), 1) == 0
    zero_pairs = lax.broadcasted_iota(jnp.int32, (pairs, HALF), 1) == 0
    sign = (1 - 2 * (lax.broadcasted_iota(jnp.int32, (pairs, LENGTH), 1) & 1)).astype(F32)
    scale = 1.0 / (LENGTH * LENGTH)
    inverse = []
    for freq in range(2):
        products = []
        for part in (2 * freq, 2 * freq + 1):
            picked = jnp.dot(pick, parts_ref[part], preferred_element_type=F32).astype(BF16)
            products.append(jnp.dot(picked, columns_ref[...], preferred_element_type=F32))
        re_cos, re_sin = products[0][:, :HALF], products[0][:, HALF:]
        im_cos, im_sin = products[1][:, :HALF], products[1][:, HALF:]
        re_odd = jnp.where(zero, 0.0, re_sin)
        im_odd = jnp.where(zero, 0.0, im_sin)
        plus = cross(re_cos + im_odd, im_cos - re_odd)
        minus = cross(
            jnp.where(zero, re_sin, re_cos - im_sin), jnp.where(zero, im_sin, im_cos + re_sin)
        )
        if freq == 0:
            low_plus = cross(re_cos, -re_odd)
            low_minus = cross(jnp.where(zero, re_sin, re_cos), re_odd)
            top_plus = cross(im_cos, -im_odd)
            top_minus = cross(jnp.where(zero, im_sin, im_cos), im_odd)
            plus = (
                jnp.where(is_first, low_plus[0] - top_plus[1], plus[0]),
                jnp.where(is_first, low_plus[1] + top_plus[0], plus[1]),
            )
            minus = (
                jnp.where(is_first, low_minus[0] - top_minus[1], minus[0]),
                jnp.where(is_first, low_minus[1] + top_minus[0], minus[1]),
            )
        even = [jnp.where(zero_pairs, plus[k], plus[k] + minus[k]) for k in range(2)]
        odd = [plus[k] - minus[k] for k in range(2)]
        even = jnp.dot(
            jnp.concatenate(even, axis=0).astype(BF16), back_ref[0], preferred_element_type=F32
        )
        odd = jnp.dot(
            jnp.concatenate(odd, axis=0).astype(BF16), back_ref[1], preferred_element_type=F32
        )
        real_cos = even[:pairs] + minus[0][:, :1] * sign
        imag_cos = even[pairs:] + minus[1][:, :1] * sign
        real_sin, imag_sin = odd[:pairs], odd[pairs:]
        own_imag = imag_cos + real_sin
        other_imag = real_sin - imag_cos
        if freq == 0:
            other_imag = jnp.where(is_first, imag_cos - real_sin, other_imag)
        inverse.append(
            (
                jnp.concatenate(
                    [real_cos - imag_sin, real_cos + imag_sin, own_imag, other_imag], axis=0
                )
                * scale
            ).astype(BF16)
        )

    blocks = 4
    count = devices // blocks
    writes = []
    for block in range(blocks):
        rows = place[block * count * 8 : (block + 1) * count * 8]
        placed = [
            split_rows(jnp.dot(rows, inverse[freq], preferred_element_type=F32), 8) for freq in range(2)
        ]
        placed = jnp.concatenate(placed, axis=1).astype(BF16)
        where = pl.ds(block * count, count)
        for lane in range(LANE_BLOCKS):
            out_ref[where, lane * 16 : (lane + 1) * 16, :] = placed[
                :, :, lane * LANES : (lane + 1) * LANES
            ]
        write = pltpu.make_async_copy(out_ref.at[where], out_hbm.at[where], out_sem.at[block])
        write.start()
        writes.append(write)
    for write in writes:
        write.wait()


def surface_kernel(count_ref, m_ref, table_ref, gather_ref, out_hbm, parts_ref, out_ref, out_sem):
    take_parts(m_ref, gather_ref[...], parts_ref)
    writes = []
    for slot in range(SLOTS_HELD):
        keep = (slot < count_ref[0]).astype(F32)
        out_ref[slot] = (
            jnp.dot(table_ref[...], parts_ref[slot], preferred_element_type=F32) * keep
        )
        write = pltpu.make_async_copy(out_ref.at[slot], out_hbm.at[0, slot], out_sem.at[slot])
        write.start()
        writes.append(write)
    for write in writes:
        write.wait()


def per_device(windows, counts, intersection_pairs):
    devices = lax.axis_size(AXES)
    position = lax.axis_index(AXES).astype(jnp.int32).reshape(1)
    forward, backward, columns, columns_back, gather = packed_tables(devices)
    smem = pl.BlockSpec(memory_space=pltpu.SMEM)
    vmem = pl.BlockSpec(memory_space=pltpu.VMEM)
    hbm = pl.BlockSpec(memory_space=pltpu.HBM)
    in_hbm = lambda x: pltpu.with_memory_space_constraint(x, pltpu.HBM)
    dma = pltpu.SemaphoreType.DMA
    params = pltpu.CompilerParams(vmem_limit_bytes=24 << 20)

    sent = pl.pallas_call(
        forward_kernel,
        in_specs=[hbm, hbm, hbm],
        out_specs=hbm,
        out_shape=pltpu.HBM((devices, CHUNK + 8, LANES), BF16),
        scratch_shapes=[
            pltpu.SMEM((1, 4), jnp.int32),
            pltpu.VMEM((SLOTS_HELD, LENGTH, LENGTH), BF16),
            pltpu.VMEM((LENGTH, LENGTH), BF16),
            pltpu.VMEM((devices, CHUNK + 8, LANES), BF16),
            dma((SLOTS_HELD,)),
            dma((2,)),
            dma((8,)),
        ],
        compiler_params=params,
        name="forward_rows",
    )(in_hbm(intersection_pairs), in_hbm(windows[0]), in_hbm(forward))
    moved = lax.all_to_all(sent, AXES, 0, 0, tiled=True)
    crossed = pl.pallas_call(
        cross_kernel,
        in_specs=[smem, vmem, vmem, vmem, vmem],
        out_specs=hbm,
        out_shape=pltpu.HBM((devices, CHUNK, LANES), BF16),
        scratch_shapes=[
            pltpu.VMEM((4, LENGTH, LENGTH), BF16),
            pltpu.VMEM((devices * 8, LANES), F32),
            pltpu.VMEM((devices, CHUNK, LANES), BF16),
            dma((4,)),
        ],
        compiler_params=params,
        name="cross_columns",
    )(position, moved, columns, columns_back, gather)
    returned = lax.all_to_all(crossed, AXES, 0, 0, tiled=True)
    return pl.pallas_call(
        surface_kernel,
        in_specs=[smem, vmem, vmem, vmem],
        out_specs=hbm,
        out_shape=pltpu.HBM((1, SLOTS_HELD, LENGTH, LENGTH), F32),
        scratch_shapes=[
            pltpu.VMEM((SLOTS_HELD, LENGTH, LENGTH), BF16),
            pltpu.VMEM((SLOTS_HELD, LENGTH, LENGTH), F32),
            dma((4,)),
        ],
        compiler_params=params,
        name="surfaces",
    )(counts, returned, backward, gather)


def solution(mesh):
    in_specs = (P(AXES, None, None, None), P(AXES), P(AXES, None))
    out_specs = P(AXES, None, None, None)
    return jax.shard_map(
        per_device, mesh=mesh, in_specs=in_specs, out_specs=out_specs, check_vma=False
    )
```

```python
import jax
import jax.numpy as jnp
import numpy as np
from jax import lax
from jax.experimental import pallas as pl
from jax.experimental.pallas import tpu as pltpu
from jax.sharding import PartitionSpec as P

AXES = ("scene", "grp")
LENGTH = 512
HALF = LENGTH // 2
SLOTS_HELD = 4
LANES = 128
LANE_BLOCKS = LENGTH // LANES
CHUNK = LANE_BLOCKS * 16
TILES = CHUNK // 2 + 1
BF16 = jnp.bfloat16
F32 = jnp.float32


def packed_tables(devices):
    places = np.arange(LENGTH)
    packed = LENGTH // devices
    forward = np.zeros((devices, packed, LENGTH))
    backward = np.zeros((devices, packed, LENGTH))
    for dev in range(devices):
        for part in range(packed):
            freq = dev * (packed // 2) + part // 2
            angle = 2.0 * np.pi * ((freq * places) % LENGTH) / LENGTH
            if part % 2 == 0:
                forward[dev, part] = np.cos(angle)
                backward[dev, part] = np.cos(angle) * (1.0 if freq == 0 else 2.0)
            elif freq == 0:
                forward[dev, part] = 1.0 - 2.0 * (places % 2)
                backward[dev, part] = 1.0 - 2.0 * (places % 2)
            else:
                forward[dev, part] = -np.sin(angle)
                backward[dev, part] = -2.0 * np.sin(angle)
    forward = forward.reshape(2, devices // 2, packed, LENGTH).transpose(1, 0, 2, 3)
    forward = forward.reshape(LENGTH, LENGTH)
    backward = backward.reshape(LENGTH, LENGTH).T / LENGTH
    product = places[:, None] * places[None, :] % LENGTH
    cosine = np.cos(2.0 * np.pi * product / LENGTH)
    sine = np.sin(2.0 * np.pi * product / LENGTH)
    packed_sine = np.concatenate([cosine[:, HALF : HALF + 1], sine[:, 1:HALF]], axis=1)
    columns = np.concatenate([cosine[:, :HALF], packed_sine], axis=1)
    columns_back = np.stack([cosine[:HALF], sine[:HALF]])
    columns_back[1, 0] = 0.0
    order = np.arange(4 * 64)
    gather = np.zeros((4 * 64, 4 * 64))
    gather[order, order % 64 * 4 + order // 64] = 1.0
    dev, slot, part = order % 64 // 4, order % 4, order // 64
    gather_slots = np.zeros((4 * 64, 4 * 64))
    gather_slots[order, slot // 2 * 128 + dev * 8 + slot % 2 * 4 + part] = 1.0
    tables = (forward, backward, columns, columns_back, gather_slots, gather)
    return tuple(jnp.asarray(table.astype(jnp.bfloat16)) for table in tables)


def split_rows(value, rows):
    return value.reshape(value.shape[0] // rows, rows, value.shape[1])


def wide(value):
    return jnp.concatenate([value] * LANE_BLOCKS, axis=1)


def total(value):
    return jnp.sum(jnp.sum(value, axis=0, keepdims=True), axis=1, keepdims=True)


def moments(x_ref, slot):
    rows = 16
    steps = LENGTH // rows
    entries = float(LENGTH * LENGTH)
    base = x_ref[slot, 0:rows, :].astype(F32)
    first = jnp.zeros_like(base)
    second = jnp.zeros_like(base)
    for step in range(1, steps):
        diff = x_ref[slot, step * rows : (step + 1) * rows, :].astype(F32) - base
        first = first + diff
        second = second + diff * diff
    local = base + first * (1.0 / steps)
    mean = total(local) * (steps / entries)
    off = local - mean
    spread = total(second - first * first * (1.0 / steps) + off * off * float(steps))
    return mean, lax.rsqrt(spread * (1.0 / entries) + 1e-05)


def forward_kernel(
    pair_hbm,
    x_hbm,
    table_hbm,
    out_hbm,
    pair_ref,
    x_ref,
    table_ref,
    out_ref,
    names_ref,
    in_sem,
    late_sem,
    out_sem,
):
    devices = out_ref.shape[0]
    groups = devices // 2
    blocks = 4
    out_rows = out_hbm.reshape(devices, 2 * TILES, LANES)
    reads = [pltpu.make_async_copy(x_hbm.at[s], x_ref.at[s], in_sem.at[s]) for s in range(SLOTS_HELD)]
    table_read = pltpu.make_async_copy(table_hbm, table_ref, late_sem.at[0])
    pair_read = pltpu.make_async_copy(pair_hbm, pair_ref, late_sem.at[1])
    reads[0].start()
    table_read.start()
    for read in reads[1:]:
        read.start()
    pair_read.start()
    ones = jnp.ones((LENGTH, LANES), BF16)
    spectra = []
    writes = []
    for s in range(SLOTS_HELD):
        reads[s].wait()
        mean, scale = moments(x_ref, s)
        if s == 0:
            table_read.wait()
            row_sum = jnp.dot(table_ref[...], ones, preferred_element_type=F32)
        product = jnp.dot(table_ref[...], x_ref[s], preferred_element_type=F32)
        spectra.append(split_rows(product * scale - wide(row_sum * (mean * scale)), 8))
        if s % 2 == 0:
            continue
        if s == 1:
            pair_read.wait()
            column = lax.broadcasted_iota(jnp.int32, (2, LANES), 1) // (LANES // 4)
            named = jnp.zeros((2, LANES), F32)
            for k in range(4):
                named = jnp.where(column == k, pair_ref[0, k].astype(F32), named)
            names_ref[...] = jnp.broadcast_to(named[None], (devices, 2, LANES)).astype(BF16)
            write = pltpu.make_async_copy(names_ref, out_hbm.at[:, TILES - 1], late_sem.at[2])
            write.start()
            writes.append(write)
        count = groups // blocks
        for block in range(blocks):
            one, two = (part[block * count : (block + 1) * count] for part in spectra[s - 1 :])
            upper = lax.broadcasted_iota(jnp.int32, one.shape, 1) < 4
            low = jnp.where(upper, one, pltpu.roll(two, 4, 1)).astype(BF16)
            high = jnp.where(upper, pltpu.roll(one, 4, 1), two).astype(BF16)
            for side, filled in enumerate((low, high)):
                place = pl.ds(side * groups + block * count, count)
                for lane in range(LANE_BLOCKS):
                    start = s // 2 * 32 + lane * 8
                    out_ref[place, start : start + 8] = filled[:, :, lane * LANES : (lane + 1) * LANES]
                rows = pl.ds(s // 2 * 32, 32)
                write = pltpu.make_async_copy(
                    out_ref.at[place, rows], out_rows.at[place, rows], out_sem.at[s // 2, 2 * block + side]
                )
                write.start()
                writes.append(write)
    for write in writes:
        write.wait()


def rows_of_16(m_ref, block):
    return jnp.concatenate(
        [
            m_ref[block * 16 : (block + 1) * 16, lane * 16 : (lane + 1) * 16, :].reshape(256, LANES)
            for lane in range(LANE_BLOCKS)
        ],
        axis=1,
    )


def rows_of_8(rows_ref, block):
    tile = lambda k: (
        rows_ref[block * 16 : (block + 1) * 16, k * 8 : (k + 1) * 8]
        .astype(F32)
        .reshape(128, LANES)
        .astype(BF16)
    )
    return jnp.concatenate(
        [
            jnp.concatenate([tile(lane), tile(LANE_BLOCKS + lane)], axis=0)
            for lane in range(LANE_BLOCKS)
        ],
        axis=1,
    )


def take_parts(m_ref, rows_of, gather, parts_ref):
    for block in range(m_ref.shape[0] // 16):
        rows = rows_of(m_ref, block)
        taken = jnp.dot(gather, rows, preferred_element_type=F32).astype(BF16)
        for part in range(4):
            parts_ref[part, block * 64 : (block + 1) * 64, :] = taken[part * 64 : (part + 1) * 64]


def cross(real, imag):
    pairs = real.shape[0] // 2
    own_real, other_real = real[:pairs], real[pairs:]
    own_imag, other_imag = imag[:pairs], imag[pairs:]
    return (
        own_real * other_real + own_imag * other_imag,
        own_imag * other_real - own_real * other_imag,
    )


def cross_kernel(
    first_ref, m_ref, columns_ref, back_ref, gather_ref, out_hbm, rows_ref, parts_ref, names_ref,
    out_ref, in_sem, out_sem
):
    devices = m_ref.shape[0]
    slots = devices * SLOTS_HELD
    pairs = devices
    is_first = first_ref[0] == 0

    copy = pltpu.make_async_copy(
        m_ref.reshape(devices, 2 * TILES, LANES).at[:, 0:CHUNK], rows_ref, in_sem.at[0]
    )
    copy.start()
    names_ref[...] = m_ref[:, TILES - 1].astype(F32).reshape(devices * 2, LANES)
    names = names_ref[pl.ds(0, devices, stride=2), :]
    named = [
        jnp.broadcast_to(names[:, k * LANES // 4 : k * LANES // 4 + 1], (devices, LANES))
        for k in range(4)
    ]
    slot_rows = [
        (named[2 * side] * SLOTS_HELD + named[2 * side + 1]).astype(jnp.int32) for side in range(2)
    ]
    same = lax.broadcasted_iota(jnp.int32, (pairs, LANES), 0) == lax.broadcasted_iota(
        jnp.int32, (pairs, LANES), 1
    )
    slot_lanes = [
        jnp.sum(jnp.where(same, slot_rows[side], 0), axis=0, keepdims=True) for side in range(2)
    ]
    wanted = jnp.concatenate([wide(slot_rows[side]) for side in range(2)], axis=0)
    pick = (wanted == lax.broadcasted_iota(jnp.int32, (2 * pairs, slots), 1)).astype(F32).astype(BF16)
    group = lax.broadcasted_iota(jnp.int32, (devices, 8, LANES), 0)
    inner = lax.broadcasted_iota(jnp.int32, (devices, 8, LANES), 1)
    row_code = (group * SLOTS_HELD + ((inner & 3) + (inner >> 2) * slots)).reshape(devices * 8, LANES)
    place = jnp.concatenate(
        [
            (row_code == slot_lanes[side] + part * slots).astype(F32).astype(BF16)
            for part in range(2)
            for side in range(2)
        ],
        axis=1,
    )
    copy.wait()
    take_parts(rows_ref, rows_of_8, gather_ref[...], parts_ref)

    zero = lax.broadcasted_iota(jnp.int32, (2 * pairs, HALF), 1) == 0
    zero_pairs = lax.broadcasted_iota(jnp.int32, (pairs, HALF), 1) == 0
    sign = (1 - 2 * (lax.broadcasted_iota(jnp.int32, (pairs, LENGTH), 1) & 1)).astype(F32)
    scale = 1.0 / (LENGTH * LENGTH)
    picked = [
        jnp.dot(pick, parts_ref[part], preferred_element_type=F32).astype(BF16) for part in range(4)
    ]
    inverse = []
    for freq in range(2):
        products = []
        for part in (2 * freq, 2 * freq + 1):
            products.append(
                jnp.dot(picked[part], columns_ref[...], preferred_element_type=F32)
            )
        re_cos, re_sin = products[0][:, :HALF], products[0][:, HALF:]
        im_cos, im_sin = products[1][:, :HALF], products[1][:, HALF:]
        re_odd = jnp.where(zero, 0.0, re_sin)
        im_odd = jnp.where(zero, 0.0, im_sin)
        plus = cross(re_cos + im_odd, im_cos - re_odd)
        minus = cross(
            jnp.where(zero, re_sin, re_cos - im_sin), jnp.where(zero, im_sin, im_cos + re_sin)
        )
        if freq == 0:
            low_plus = cross(re_cos, -re_odd)
            low_minus = cross(jnp.where(zero, re_sin, re_cos), re_odd)
            top_plus = cross(im_cos, -im_odd)
            top_minus = cross(jnp.where(zero, im_sin, im_cos), im_odd)
            plus = (
                jnp.where(is_first, low_plus[0] - top_plus[1], plus[0]),
                jnp.where(is_first, low_plus[1] + top_plus[0], plus[1]),
            )
            minus = (
                jnp.where(is_first, low_minus[0] - top_minus[1], minus[0]),
                jnp.where(is_first, low_minus[1] + top_minus[0], minus[1]),
            )
        even = [jnp.where(zero_pairs, plus[k], plus[k] + minus[k]) for k in range(2)]
        odd = [plus[k] - minus[k] for k in range(2)]
        even = jnp.dot(
            jnp.concatenate(even, axis=0).astype(BF16), back_ref[0], preferred_element_type=F32
        )
        odd = jnp.dot(
            jnp.concatenate(odd, axis=0).astype(BF16), back_ref[1], preferred_element_type=F32
        )
        real_cos = even[:pairs] + minus[0][:, :1] * sign
        imag_cos = even[pairs:] + minus[1][:, :1] * sign
        real_sin, imag_sin = odd[:pairs], odd[pairs:]
        own_imag = imag_cos + real_sin
        other_imag = real_sin - imag_cos
        if freq == 0:
            other_imag = jnp.where(is_first, imag_cos - real_sin, other_imag)
        inverse.append(
            (
                jnp.concatenate(
                    [real_cos - imag_sin, real_cos + imag_sin, own_imag, other_imag], axis=0
                )
                * scale
            ).astype(BF16)
        )

    blocks = 4
    count = devices // blocks
    writes = []
    for block in range(blocks):
        rows = place[block * count * 8 : (block + 1) * count * 8]
        placed = [
            split_rows(jnp.dot(rows, inverse[freq], preferred_element_type=F32), 8) for freq in range(2)
        ]
        placed = jnp.concatenate(placed, axis=1).astype(BF16)
        where = pl.ds(block * count, count)
        for lane in range(LANE_BLOCKS):
            out_ref[where, lane * 16 : (lane + 1) * 16, :] = placed[
                :, :, lane * LANES : (lane + 1) * LANES
            ]
        write = pltpu.make_async_copy(out_ref.at[where], out_hbm.at[where], out_sem.at[block])
        write.start()
        writes.append(write)
    for write in writes:
        write.wait()


def surface_kernel(count_ref, m_ref, table_ref, gather_ref, out_hbm, parts_ref, out_ref, out_sem):
    take_parts(m_ref, rows_of_16, gather_ref[...], parts_ref)
    writes = []
    for slot in range(SLOTS_HELD):
        keep = (slot < count_ref[0]).astype(F32)
        out_ref[slot] = (
            jnp.dot(table_ref[...], parts_ref[slot], preferred_element_type=F32) * keep
        )
        write = pltpu.make_async_copy(out_ref.at[slot], out_hbm.at[0, slot], out_sem.at[slot])
        write.start()
        writes.append(write)
    for write in writes:
        write.wait()


def per_device(windows, counts, intersection_pairs):
    devices = lax.axis_size(AXES)
    position = lax.axis_index(AXES).astype(jnp.int32).reshape(1)
    forward, backward, columns, columns_back, gather_slots, gather = packed_tables(devices)
    smem = pl.BlockSpec(memory_space=pltpu.SMEM)
    vmem = pl.BlockSpec(memory_space=pltpu.VMEM)
    hbm = pl.BlockSpec(memory_space=pltpu.HBM)
    in_hbm = lambda x: pltpu.with_memory_space_constraint(x, pltpu.HBM)
    dma = pltpu.SemaphoreType.DMA
    params = pltpu.CompilerParams(vmem_limit_bytes=24 << 20)

    sent = pl.pallas_call(
        forward_kernel,
        in_specs=[hbm, hbm, hbm],
        out_specs=hbm,
        out_shape=pltpu.HBM((devices, TILES, 2, LANES), BF16),
        scratch_shapes=[
            pltpu.SMEM((1, 4), jnp.int32),
            pltpu.VMEM((SLOTS_HELD, LENGTH, LENGTH), BF16),
            pltpu.VMEM((LENGTH, LENGTH), BF16),
            pltpu.VMEM((devices, CHUNK, LANES), BF16),
            pltpu.VMEM((devices, 2, LANES), BF16),
            dma((SLOTS_HELD,)),
            dma((3,)),
            dma((2, 8)),
        ],
        compiler_params=params,
        name="forward_rows",
    )(in_hbm(intersection_pairs), in_hbm(windows[0]), in_hbm(forward))
    moved = lax.all_to_all(sent, AXES, 0, 0, tiled=True)
    crossed = pl.pallas_call(
        cross_kernel,
        in_specs=[smem, vmem, vmem, vmem, vmem],
        out_specs=hbm,
        out_shape=pltpu.HBM((devices, CHUNK, LANES), BF16),
        scratch_shapes=[
            pltpu.VMEM((devices, CHUNK, LANES), BF16),
            pltpu.VMEM((4, LENGTH, LENGTH), BF16),
            pltpu.VMEM((devices * 2, LANES), F32),
            pltpu.VMEM((devices, CHUNK, LANES), BF16),
            dma((1,)),
            dma((4,)),
        ],
        compiler_params=params,
        name="cross_columns",
    )(position, moved, columns, columns_back, gather_slots)
    returned = lax.all_to_all(crossed, AXES, 0, 0, tiled=True)
    return pl.pallas_call(
        surface_kernel,
        in_specs=[smem, vmem, vmem, vmem],
        out_specs=hbm,
        out_shape=pltpu.HBM((1, SLOTS_HELD, LENGTH, LENGTH), F32),
        scratch_shapes=[
            pltpu.VMEM((SLOTS_HELD, LENGTH, LENGTH), BF16),
            pltpu.VMEM((SLOTS_HELD, LENGTH, LENGTH), F32),
            dma((4,)),
        ],
        compiler_params=params,
        name="surfaces",
    )(counts, returned, backward, gather)


def solution(mesh):
    in_specs = (P(AXES, None, None, None), P(AXES), P(AXES, None))
    out_specs = P(AXES, None, None, None)
    return jax.shard_map(
        per_device, mesh=mesh, in_specs=in_specs, out_specs=out_specs, check_vma=False
    )
```

```python
import jax
import jax.numpy as jnp
import numpy as np
from jax import lax
from jax.experimental import pallas as pl
from jax.experimental.pallas import tpu as pltpu
from jax.sharding import PartitionSpec as P

AXES = ("scene", "grp")
LENGTH = 512
HALF = LENGTH // 2
SLOTS_HELD = 4
LANES = 128
LANE_BLOCKS = LENGTH // LANES
CHUNK = LANE_BLOCKS * 16
TILES = CHUNK // 2 + 1
BF16 = jnp.bfloat16
F32 = jnp.float32


def packed_tables(devices):
    places = np.arange(LENGTH)
    packed = LENGTH // devices
    forward = np.zeros((devices, packed, LENGTH))
    backward = np.zeros((devices, packed, LENGTH))
    for dev in range(devices):
        for part in range(packed):
            freq = dev * (packed // 2) + part // 2
            angle = 2.0 * np.pi * ((freq * places) % LENGTH) / LENGTH
            if part % 2 == 0:
                forward[dev, part] = np.cos(angle)
                backward[dev, part] = np.cos(angle) * (1.0 if freq == 0 else 2.0)
            elif freq == 0:
                forward[dev, part] = 1.0 - 2.0 * (places % 2)
                backward[dev, part] = 1.0 - 2.0 * (places % 2)
            else:
                forward[dev, part] = -np.sin(angle)
                backward[dev, part] = -2.0 * np.sin(angle)
    forward = forward.reshape(2, devices // 2, packed, LENGTH).transpose(1, 0, 2, 3)
    forward = forward.reshape(LENGTH, LENGTH)
    backward = backward.reshape(LENGTH, LENGTH).T / LENGTH
    product = places[:, None] * places[None, :] % LENGTH
    cosine = np.cos(2.0 * np.pi * product / LENGTH)
    sine = np.sin(2.0 * np.pi * product / LENGTH)
    packed_sine = np.concatenate([cosine[:, HALF : HALF + 1], sine[:, 1:HALF]], axis=1)
    columns = np.concatenate([cosine[:, :HALF], packed_sine], axis=1)
    columns_back = np.stack([cosine[:HALF], sine[:HALF]])
    columns_back[1, 0] = 0.0
    order = np.arange(4 * 64)
    gather = np.zeros((4 * 64, 4 * 64))
    gather[order, order % 64 * 4 + order // 64] = 1.0
    dev, slot, part = order % 64 // 4, order % 4, order // 64
    gather_slots = np.zeros((4 * 64, 4 * 64))
    gather_slots[order, slot // 2 * 128 + dev * 8 + slot % 2 * 4 + part] = 1.0
    tables = (forward, backward, columns, columns_back, gather_slots, gather)
    return tuple(jnp.asarray(table.astype(jnp.bfloat16)) for table in tables)


def split_rows(value, rows):
    return value.reshape(value.shape[0] // rows, rows, value.shape[1])


def wide(value):
    return jnp.concatenate([value] * LANE_BLOCKS, axis=1)


def total(value):
    return jnp.sum(jnp.sum(value, axis=0, keepdims=True), axis=1, keepdims=True)


def moments(x_ref, slot):
    rows = 16
    steps = LENGTH // rows
    entries = float(LENGTH * LENGTH)
    base = x_ref[slot, 0:rows, :].astype(F32)
    first = jnp.zeros_like(base)
    second = jnp.zeros_like(base)
    for step in range(1, steps):
        diff = x_ref[slot, step * rows : (step + 1) * rows, :].astype(F32) - base
        first = first + diff
        second = second + diff * diff
    local = base + first * (1.0 / steps)
    mean = total(local) * (steps / entries)
    off = local - mean
    spread = total(second - first * first * (1.0 / steps) + off * off * float(steps))
    return mean, lax.rsqrt(spread * (1.0 / entries) + 1e-05)


def forward_kernel(
    pair_hbm,
    x_hbm,
    table_hbm,
    out_hbm,
    pair_ref,
    x_ref,
    table_ref,
    out_ref,
    names_ref,
    in_sem,
    late_sem,
    out_sem,
):
    devices = out_ref.shape[0]
    groups = devices // 2
    blocks = 8
    out_rows = out_hbm.reshape(devices, 2 * TILES, LANES)
    reads = [pltpu.make_async_copy(x_hbm.at[s], x_ref.at[s], in_sem.at[s]) for s in range(SLOTS_HELD)]
    table_read = pltpu.make_async_copy(table_hbm, table_ref, late_sem.at[0])
    pair_read = pltpu.make_async_copy(pair_hbm, pair_ref, late_sem.at[1])
    reads[0].start()
    table_read.start()
    for read in reads[1:]:
        read.start()
    pair_read.start()
    ones = jnp.ones((LENGTH, LANES), BF16)
    spectra = []
    writes = []
    for s in range(SLOTS_HELD):
        reads[s].wait()
        mean, scale = moments(x_ref, s)
        if s == 0:
            table_read.wait()
            row_sum = jnp.dot(table_ref[...], ones, preferred_element_type=F32)
        product = jnp.dot(table_ref[...], x_ref[s], preferred_element_type=F32)
        spectra.append(split_rows(product * scale - wide(row_sum * (mean * scale)), 8))
        if s % 2 == 0:
            continue
        if s == 1:
            pair_read.wait()
            column = lax.broadcasted_iota(jnp.int32, (2, LANES), 1) // (LANES // 4)
            named = jnp.zeros((2, LANES), F32)
            for k in range(4):
                named = jnp.where(column == k, pair_ref[0, k].astype(F32), named)
            names_ref[...] = jnp.broadcast_to(named[None], (devices, 2, LANES)).astype(BF16)
            write = pltpu.make_async_copy(names_ref, out_hbm.at[:, TILES - 1], late_sem.at[2])
            write.start()
            writes.append(write)
        count = groups // blocks
        for block in range(blocks):
            one, two = (part[block * count : (block + 1) * count] for part in spectra[s - 1 :])
            upper = lax.broadcasted_iota(jnp.int32, one.shape, 1) < 4
            low = jnp.where(upper, one, pltpu.roll(two, 4, 1)).astype(BF16)
            high = jnp.where(upper, pltpu.roll(one, 4, 1), two).astype(BF16)
            for side, filled in enumerate((low, high)):
                place = pl.ds(side * groups + block * count, count)
                for lane in range(LANE_BLOCKS):
                    start = s // 2 * 32 + lane * 8
                    out_ref[place, start : start + 8] = filled[:, :, lane * LANES : (lane + 1) * LANES]
                rows = pl.ds(s // 2 * 32, 32)
                write = pltpu.make_async_copy(
                    out_ref.at[place, rows], out_rows.at[place, rows], out_sem.at[s // 2, 2 * block + side]
                )
                write.start()
                writes.append(write)
    for write in writes:
        write.wait()


def rows_of_16(m_ref, block):
    return jnp.concatenate(
        [
            m_ref[block * 16 : (block + 1) * 16, lane * 16 : (lane + 1) * 16, :].reshape(256, LANES)
            for lane in range(LANE_BLOCKS)
        ],
        axis=1,
    )


def rows_of_8(rows_ref, block):
    tile = lambda k: (
        rows_ref[block * 16 : (block + 1) * 16, k * 8 : (k + 1) * 8]
        .astype(F32)
        .reshape(128, LANES)
        .astype(BF16)
    )
    return jnp.concatenate(
        [
            jnp.concatenate([tile(lane), tile(LANE_BLOCKS + lane)], axis=0)
            for lane in range(LANE_BLOCKS)
        ],
        axis=1,
    )


def take_parts(m_ref, rows_of, gather, parts_ref):
    for block in range(m_ref.shape[0] // 16):
        rows = rows_of(m_ref, block)
        taken = jnp.dot(gather, rows, preferred_element_type=F32).astype(BF16)
        for part in range(4):
            parts_ref[part, block * 64 : (block + 1) * 64, :] = taken[part * 64 : (part + 1) * 64]


def cross(real, imag):
    pairs = real.shape[0] // 2
    own_real, other_real = real[:pairs], real[pairs:]
    own_imag, other_imag = imag[:pairs], imag[pairs:]
    return (
        own_real * other_real + own_imag * other_imag,
        own_imag * other_real - own_real * other_imag,
    )


def cross_kernel(
    first_ref, m_ref, columns_ref, back_ref, gather_ref, out_hbm, rows_ref, parts_ref, names_ref,
    out_ref, in_sem, out_sem
):
    devices = m_ref.shape[0]
    slots = devices * SLOTS_HELD
    pairs = devices
    is_first = first_ref[0] == 0

    copy = pltpu.make_async_copy(
        m_ref.reshape(devices, 2 * TILES, LANES).at[:, 0:CHUNK], rows_ref, in_sem.at[0]
    )
    copy.start()
    names_ref[...] = m_ref[:, TILES - 1].astype(F32).reshape(devices * 2, LANES)
    names = names_ref[pl.ds(0, devices, stride=2), :]
    named = [
        jnp.broadcast_to(names[:, k * LANES // 4 : k * LANES // 4 + 1], (devices, LANES))
        for k in range(4)
    ]
    slot_rows = [
        (named[2 * side] * SLOTS_HELD + named[2 * side + 1]).astype(jnp.int32) for side in range(2)
    ]
    same = lax.broadcasted_iota(jnp.int32, (pairs, LANES), 0) == lax.broadcasted_iota(
        jnp.int32, (pairs, LANES), 1
    )
    slot_lanes = [
        jnp.sum(jnp.where(same, slot_rows[side], 0), axis=0, keepdims=True) for side in range(2)
    ]
    wanted = jnp.concatenate([wide(slot_rows[side]) for side in range(2)], axis=0)
    pick = (wanted == lax.broadcasted_iota(jnp.int32, (2 * pairs, slots), 1)).astype(F32).astype(BF16)
    group = lax.broadcasted_iota(jnp.int32, (devices, 8, LANES), 0)
    inner = lax.broadcasted_iota(jnp.int32, (devices, 8, LANES), 1)
    row_code = (group * SLOTS_HELD + ((inner & 3) + (inner >> 2) * slots)).reshape(devices * 8, LANES)
    place = jnp.concatenate(
        [
            (row_code == slot_lanes[side] + part * slots).astype(F32).astype(BF16)
            for part in range(2)
            for side in range(2)
        ],
        axis=1,
    )
    copy.wait()
    take_parts(rows_ref, rows_of_8, gather_ref[...], parts_ref)

    zero = lax.broadcasted_iota(jnp.int32, (2 * pairs, HALF), 1) == 0
    zero_pairs = lax.broadcasted_iota(jnp.int32, (pairs, HALF), 1) == 0
    sign = (1 - 2 * (lax.broadcasted_iota(jnp.int32, (pairs, LENGTH), 1) & 1)).astype(F32)
    scale = 1.0 / (LENGTH * LENGTH)
    picked = [
        jnp.dot(pick, parts_ref[part], preferred_element_type=F32).astype(BF16) for part in range(4)
    ]
    spectra = jnp.dot(
        jnp.concatenate(picked, axis=0), columns_ref[...], preferred_element_type=F32
    )
    inverse = []
    for freq in range(2):
        products = [
            spectra[part * 2 * pairs : (part + 1) * 2 * pairs] for part in (2 * freq, 2 * freq + 1)
        ]
        re_cos, re_sin = products[0][:, :HALF], products[0][:, HALF:]
        im_cos, im_sin = products[1][:, :HALF], products[1][:, HALF:]
        re_odd = jnp.where(zero, 0.0, re_sin)
        im_odd = jnp.where(zero, 0.0, im_sin)
        plus = cross(re_cos + im_odd, im_cos - re_odd)
        minus = cross(
            jnp.where(zero, re_sin, re_cos - im_sin), jnp.where(zero, im_sin, im_cos + re_sin)
        )
        if freq == 0:
            low_plus = cross(re_cos, -re_odd)
            low_minus = cross(jnp.where(zero, re_sin, re_cos), re_odd)
            top_plus = cross(im_cos, -im_odd)
            top_minus = cross(jnp.where(zero, im_sin, im_cos), im_odd)
            plus = (
                jnp.where(is_first, low_plus[0] - top_plus[1], plus[0]),
                jnp.where(is_first, low_plus[1] + top_plus[0], plus[1]),
            )
            minus = (
                jnp.where(is_first, low_minus[0] - top_minus[1], minus[0]),
                jnp.where(is_first, low_minus[1] + top_minus[0], minus[1]),
            )
        even = [jnp.where(zero_pairs, plus[k], plus[k] + minus[k]) for k in range(2)]
        odd = [plus[k] - minus[k] for k in range(2)]
        even = jnp.dot(
            jnp.concatenate(even, axis=0).astype(BF16), back_ref[0], preferred_element_type=F32
        )
        odd = jnp.dot(
            jnp.concatenate(odd, axis=0).astype(BF16), back_ref[1], preferred_element_type=F32
        )
        real_cos = even[:pairs] + minus[0][:, :1] * sign
        imag_cos = even[pairs:] + minus[1][:, :1] * sign
        real_sin, imag_sin = odd[:pairs], odd[pairs:]
        own_imag = imag_cos + real_sin
        other_imag = real_sin - imag_cos
        if freq == 0:
            other_imag = jnp.where(is_first, imag_cos - real_sin, other_imag)
        inverse.append(
            (
                jnp.concatenate(
                    [real_cos - imag_sin, real_cos + imag_sin, own_imag, other_imag], axis=0
                )
                * scale
            ).astype(BF16)
        )

    blocks = 4
    count = devices // blocks
    writes = []
    for block in range(blocks):
        rows = place[block * count * 8 : (block + 1) * count * 8]
        placed = [
            split_rows(jnp.dot(rows, inverse[freq], preferred_element_type=F32), 8) for freq in range(2)
        ]
        placed = jnp.concatenate(placed, axis=1).astype(BF16)
        where = pl.ds(block * count, count)
        for lane in range(LANE_BLOCKS):
            out_ref[where, lane * 16 : (lane + 1) * 16, :] = placed[
                :, :, lane * LANES : (lane + 1) * LANES
            ]
        write = pltpu.make_async_copy(out_ref.at[where], out_hbm.at[where], out_sem.at[block])
        write.start()
        writes.append(write)
    for write in writes:
        write.wait()


def surface_kernel(count_ref, m_ref, table_ref, gather_ref, out_hbm, parts_ref, out_ref, out_sem):
    take_parts(m_ref, rows_of_16, gather_ref[...], parts_ref)
    writes = []
    parts = 2
    for slot in range(SLOTS_HELD):
        keep = (slot < count_ref[0]).astype(F32)
        for part in range(parts):
            rows = pl.ds(part * LENGTH // parts, LENGTH // parts)
            out_ref[slot, rows] = (
                jnp.dot(table_ref[rows], parts_ref[slot], preferred_element_type=F32) * keep
            )
            write = pltpu.make_async_copy(
                out_ref.at[slot, rows], out_hbm.at[0, slot, rows], out_sem.at[slot, part]
            )
            write.start()
            writes.append(write)
    for write in writes:
        write.wait()


def per_device(windows, counts, intersection_pairs):
    devices = lax.axis_size(AXES)
    position = lax.axis_index(AXES).astype(jnp.int32).reshape(1)
    forward, backward, columns, columns_back, gather_slots, gather = packed_tables(devices)
    smem = pl.BlockSpec(memory_space=pltpu.SMEM)
    vmem = pl.BlockSpec(memory_space=pltpu.VMEM)
    hbm = pl.BlockSpec(memory_space=pltpu.HBM)
    in_hbm = lambda x: pltpu.with_memory_space_constraint(x, pltpu.HBM)
    dma = pltpu.SemaphoreType.DMA
    params = pltpu.CompilerParams(vmem_limit_bytes=24 << 20)

    sent = pl.pallas_call(
        forward_kernel,
        in_specs=[hbm, hbm, hbm],
        out_specs=hbm,
        out_shape=pltpu.HBM((devices, TILES, 2, LANES), BF16),
        scratch_shapes=[
            pltpu.SMEM((1, 4), jnp.int32),
            pltpu.VMEM((SLOTS_HELD, LENGTH, LENGTH), BF16),
            pltpu.VMEM((LENGTH, LENGTH), BF16),
            pltpu.VMEM((devices, CHUNK, LANES), BF16),
            pltpu.VMEM((devices, 2, LANES), BF16),
            dma((SLOTS_HELD,)),
            dma((3,)),
            dma((2, 16)),
        ],
        compiler_params=params,
        name="forward_rows",
    )(in_hbm(intersection_pairs), in_hbm(windows[0]), in_hbm(forward))
    moved = lax.all_to_all(sent, AXES, 0, 0, tiled=True)
    crossed = pl.pallas_call(
        cross_kernel,
        in_specs=[smem, vmem, vmem, vmem, vmem],
        out_specs=hbm,
        out_shape=pltpu.HBM((devices, CHUNK, LANES), BF16),
        scratch_shapes=[
            pltpu.VMEM((devices, CHUNK, LANES), BF16),
            pltpu.VMEM((4, LENGTH, LENGTH), BF16),
            pltpu.VMEM((devices * 2, LANES), F32),
            pltpu.VMEM((devices, CHUNK, LANES), BF16),
            dma((1,)),
            dma((4,)),
        ],
        compiler_params=params,
        name="cross_columns",
    )(position, moved, columns, columns_back, gather_slots)
    returned = lax.all_to_all(crossed, AXES, 0, 0, tiled=True)
    return pl.pallas_call(
        surface_kernel,
        in_specs=[smem, vmem, vmem, vmem],
        out_specs=hbm,
        out_shape=pltpu.HBM((1, SLOTS_HELD, LENGTH, LENGTH), F32),
        scratch_shapes=[
            pltpu.VMEM((SLOTS_HELD, LENGTH, LENGTH), BF16),
            pltpu.VMEM((SLOTS_HELD, LENGTH, LENGTH), F32),
            dma((4, 2)),
        ],
        compiler_params=params,
        name="surfaces",
    )(counts, returned, backward, gather)


def solution(mesh):
    in_specs = (P(AXES, None, None, None), P(AXES), P(AXES, None))
    out_specs = P(AXES, None, None, None)
    return jax.shard_map(
        per_device, mesh=mesh, in_specs=in_specs, out_specs=out_specs, check_vma=False
    )
```

```python
import jax
import jax.numpy as jnp
import numpy as np
from jax import lax
from jax.experimental import pallas as pl
from jax.experimental.pallas import tpu as pltpu
from jax.sharding import Mesh
from jax.sharding import PartitionSpec as P

AXES = ("x", "y", "core", "z")
SIZES = (4, 4, 2, 4)
ORDER = ("core", "z", "y", "x")
LENGTH = 512
HALF = LENGTH // 2
SLOTS_HELD = 4
LANES = 128
LANE_BLOCKS = LENGTH // LANES
CHUNK = LANE_BLOCKS * 16
TILES = CHUNK // 2 + 1
BF16 = jnp.bfloat16
F32 = jnp.float32


def packed_tables(devices):
    places = np.arange(LENGTH)
    packed = LENGTH // devices
    forward = np.zeros((devices, packed, LENGTH))
    backward = np.zeros((devices, packed, LENGTH))
    for dev in range(devices):
        for part in range(packed):
            freq = dev * (packed // 2) + part // 2
            angle = 2.0 * np.pi * ((freq * places) % LENGTH) / LENGTH
            if part % 2 == 0:
                forward[dev, part] = np.cos(angle)
                backward[dev, part] = np.cos(angle) * (1.0 if freq == 0 else 2.0)
            elif freq == 0:
                forward[dev, part] = 1.0 - 2.0 * (places % 2)
                backward[dev, part] = 1.0 - 2.0 * (places % 2)
            else:
                forward[dev, part] = -np.sin(angle)
                backward[dev, part] = -2.0 * np.sin(angle)
    forward = forward.reshape(2, devices // 2, packed, LENGTH).transpose(1, 0, 2, 3)
    forward = forward.reshape(LENGTH, LENGTH)
    backward = backward.reshape(LENGTH, LENGTH).T / LENGTH
    product = places[:, None] * places[None, :] % LENGTH
    cosine = np.cos(2.0 * np.pi * product / LENGTH)
    sine = np.sin(2.0 * np.pi * product / LENGTH)
    packed_sine = np.concatenate([cosine[:, HALF : HALF + 1], sine[:, 1:HALF]], axis=1)
    columns = np.concatenate([cosine[:, :HALF], packed_sine], axis=1)
    columns_back = np.stack([cosine[:HALF], sine[:HALF]])
    columns_back[1, 0] = 0.0
    order = np.arange(4 * 64)
    gather = np.zeros((4 * 64, 4 * 64))
    gather[order, order % 64 * 4 + order // 64] = 1.0
    dev, slot, part = order % 64 // 4, order % 4, order // 64
    gather_slots = np.zeros((4 * 64, 4 * 64))
    gather_slots[order, slot // 2 * 128 + dev * 8 + slot % 2 * 4 + part] = 1.0
    tables = (forward, backward, columns, columns_back, gather_slots, gather)
    return tuple(jnp.asarray(table.astype(jnp.bfloat16)) for table in tables)


def split_rows(value, rows):
    return value.reshape(value.shape[0] // rows, rows, value.shape[1])


def wide(value):
    return jnp.concatenate([value] * LANE_BLOCKS, axis=1)


def total(value):
    return jnp.sum(jnp.sum(value, axis=0, keepdims=True), axis=1, keepdims=True)


def moments(x_ref, slot):
    rows = 16
    steps = LENGTH // rows
    entries = float(LENGTH * LENGTH)
    base = x_ref[slot, 0:rows, :].astype(F32)
    first = jnp.zeros_like(base)
    second = jnp.zeros_like(base)
    for step in range(1, steps):
        diff = x_ref[slot, step * rows : (step + 1) * rows, :].astype(F32) - base
        first = first + diff
        second = second + diff * diff
    local = base + first * (1.0 / steps)
    mean = total(local) * (steps / entries)
    off = local - mean
    spread = total(second - first * first * (1.0 / steps) + off * off * float(steps))
    return mean, lax.rsqrt(spread * (1.0 / entries) + 1e-05)


def exchange_place(scene):
    z, core, y, x = scene & 3, (scene >> 2) & 1, (scene >> 3) & 3, scene >> 5
    return ((core * 4 + z) * 4 + y) * 4 + x


def forward_kernel(
    pair_hbm,
    x_hbm,
    table_hbm,
    out_hbm,
    pair_ref,
    x_ref,
    table_ref,
    out_ref,
    names_ref,
    in_sem,
    late_sem,
    out_sem,
):
    devices = out_ref.shape[0]
    groups = devices // 2
    blocks = 8
    out_rows = out_hbm.reshape(devices, 2 * TILES, LANES)
    reads = [pltpu.make_async_copy(x_hbm.at[s], x_ref.at[s], in_sem.at[s]) for s in range(SLOTS_HELD)]
    table_read = pltpu.make_async_copy(table_hbm, table_ref, late_sem.at[0])
    pair_read = pltpu.make_async_copy(pair_hbm, pair_ref, late_sem.at[1])
    reads[0].start()
    table_read.start()
    for read in reads[1:]:
        read.start()
    pair_read.start()
    ones = jnp.ones((LENGTH, LANES), BF16)
    spectra = []
    writes = []
    for s in range(SLOTS_HELD):
        reads[s].wait()
        mean, scale = moments(x_ref, s)
        if s == 0:
            table_read.wait()
            row_sum = jnp.dot(table_ref[...], ones, preferred_element_type=F32)
        product = jnp.dot(table_ref[...], x_ref[s], preferred_element_type=F32)
        spectra.append(split_rows(product * scale - wide(row_sum * (mean * scale)), 8))
        if s % 2 == 0:
            continue
        if s == 1:
            pair_read.wait()
            column = lax.broadcasted_iota(jnp.int32, (2, LANES), 1) // (LANES // 4)
            named = jnp.zeros((2, LANES), F32)
            for k in range(4):
                value = pair_ref[0, k] if k % 2 else exchange_place(pair_ref[0, k])
                named = jnp.where(column == k, value.astype(F32), named)
            names_ref[...] = jnp.broadcast_to(named[None], (devices, 2, LANES)).astype(BF16)
            write = pltpu.make_async_copy(names_ref, out_hbm.at[:, TILES - 1], late_sem.at[2])
            write.start()
            writes.append(write)
        count = groups // blocks
        for block in range(blocks):
            one, two = (part[block * count : (block + 1) * count] for part in spectra[s - 1 :])
            upper = lax.broadcasted_iota(jnp.int32, one.shape, 1) < 4
            low = jnp.where(upper, one, pltpu.roll(two, 4, 1)).astype(BF16)
            high = jnp.where(upper, pltpu.roll(one, 4, 1), two).astype(BF16)
            for side, filled in enumerate((low, high)):
                place = pl.ds(side * groups + block * count, count)
                for lane in range(LANE_BLOCKS):
                    start = s // 2 * 32 + lane * 8
                    out_ref[place, start : start + 8] = filled[:, :, lane * LANES : (lane + 1) * LANES]
                rows = pl.ds(s // 2 * 32, 32)
                write = pltpu.make_async_copy(
                    out_ref.at[place, rows], out_rows.at[place, rows], out_sem.at[s // 2, 2 * block + side]
                )
                write.start()
                writes.append(write)
    for write in writes:
        write.wait()


def rows_of_16(m_ref, block):
    return jnp.concatenate(
        [
            m_ref[block * 16 : (block + 1) * 16, lane * 16 : (lane + 1) * 16, :].reshape(256, LANES)
            for lane in range(LANE_BLOCKS)
        ],
        axis=1,
    )


def rows_of_8(rows_ref, block):
    tile = lambda k: (
        rows_ref[block * 16 : (block + 1) * 16, k * 8 : (k + 1) * 8]
        .astype(F32)
        .reshape(128, LANES)
        .astype(BF16)
    )
    return jnp.concatenate(
        [
            jnp.concatenate([tile(lane), tile(LANE_BLOCKS + lane)], axis=0)
            for lane in range(LANE_BLOCKS)
        ],
        axis=1,
    )


def take_parts(m_ref, rows_of, gather, parts_ref):
    for block in range(m_ref.shape[0] // 16):
        rows = rows_of(m_ref, block)
        taken = jnp.dot(gather, rows, preferred_element_type=F32).astype(BF16)
        for part in range(4):
            parts_ref[part, block * 64 : (block + 1) * 64, :] = taken[part * 64 : (part + 1) * 64]


def cross(real, imag):
    pairs = real.shape[0] // 2
    own_real, other_real = real[:pairs], real[pairs:]
    own_imag, other_imag = imag[:pairs], imag[pairs:]
    return (
        own_real * other_real + own_imag * other_imag,
        own_imag * other_real - own_real * other_imag,
    )


def cross_kernel(
    first_ref, m_ref, columns_ref, back_ref, gather_ref, out_hbm, rows_ref, parts_ref, names_ref,
    out_ref, in_sem, out_sem
):
    devices = m_ref.shape[0]
    slots = devices * SLOTS_HELD
    pairs = devices
    is_first = first_ref[0] == 0

    copy = pltpu.make_async_copy(
        m_ref.reshape(devices, 2 * TILES, LANES).at[:, 0:CHUNK], rows_ref, in_sem.at[0]
    )
    copy.start()
    names_ref[...] = m_ref[:, TILES - 1].astype(F32).reshape(devices * 2, LANES)
    names = names_ref[pl.ds(0, devices, stride=2), :]
    named = [
        jnp.broadcast_to(names[:, k * LANES // 4 : k * LANES // 4 + 1], (devices, LANES))
        for k in range(4)
    ]
    slot_rows = [
        (named[2 * side] * SLOTS_HELD + named[2 * side + 1]).astype(jnp.int32) for side in range(2)
    ]
    same = lax.broadcasted_iota(jnp.int32, (pairs, LANES), 0) == lax.broadcasted_iota(
        jnp.int32, (pairs, LANES), 1
    )
    slot_lanes = [
        jnp.sum(jnp.where(same, slot_rows[side], 0), axis=0, keepdims=True) for side in range(2)
    ]
    wanted = jnp.concatenate([wide(slot_rows[side]) for side in range(2)], axis=0)
    pick = (wanted == lax.broadcasted_iota(jnp.int32, (2 * pairs, slots), 1)).astype(F32).astype(BF16)
    group = lax.broadcasted_iota(jnp.int32, (devices, 8, LANES), 0)
    inner = lax.broadcasted_iota(jnp.int32, (devices, 8, LANES), 1)
    row_code = (group * SLOTS_HELD + ((inner & 3) + (inner >> 2) * slots)).reshape(devices * 8, LANES)
    place = jnp.concatenate(
        [
            (row_code == slot_lanes[side] + part * slots).astype(F32).astype(BF16)
            for part in range(2)
            for side in range(2)
        ],
        axis=1,
    )
    copy.wait()
    take_parts(rows_ref, rows_of_8, gather_ref[...], parts_ref)

    zero = lax.broadcasted_iota(jnp.int32, (2 * pairs, HALF), 1) == 0
    zero_pairs = lax.broadcasted_iota(jnp.int32, (pairs, HALF), 1) == 0
    sign = (1 - 2 * (lax.broadcasted_iota(jnp.int32, (pairs, LENGTH), 1) & 1)).astype(F32)
    scale = 1.0 / (LENGTH * LENGTH)
    picked = [
        jnp.dot(pick, parts_ref[part], preferred_element_type=F32).astype(BF16) for part in range(4)
    ]
    spectra = jnp.dot(
        jnp.concatenate(picked, axis=0), columns_ref[...], preferred_element_type=F32
    )
    inverse = []
    for freq in range(2):
        products = [
            spectra[part * 2 * pairs : (part + 1) * 2 * pairs] for part in (2 * freq, 2 * freq + 1)
        ]
        re_cos, re_sin = products[0][:, :HALF], products[0][:, HALF:]
        im_cos, im_sin = products[1][:, :HALF], products[1][:, HALF:]
        re_odd = jnp.where(zero, 0.0, re_sin)
        im_odd = jnp.where(zero, 0.0, im_sin)
        plus = cross(re_cos + im_odd, im_cos - re_odd)
        minus = cross(
            jnp.where(zero, re_sin, re_cos - im_sin), jnp.where(zero, im_sin, im_cos + re_sin)
        )
        if freq == 0:
            low_plus = cross(re_cos, -re_odd)
            low_minus = cross(jnp.where(zero, re_sin, re_cos), re_odd)
            top_plus = cross(im_cos, -im_odd)
            top_minus = cross(jnp.where(zero, im_sin, im_cos), im_odd)
            plus = (
                jnp.where(is_first, low_plus[0] - top_plus[1], plus[0]),
                jnp.where(is_first, low_plus[1] + top_plus[0], plus[1]),
            )
            minus = (
                jnp.where(is_first, low_minus[0] - top_minus[1], minus[0]),
                jnp.where(is_first, low_minus[1] + top_minus[0], minus[1]),
            )
        even = [jnp.where(zero_pairs, plus[k], plus[k] + minus[k]) for k in range(2)]
        odd = [plus[k] - minus[k] for k in range(2)]
        even = jnp.dot(
            jnp.concatenate(even, axis=0).astype(BF16), back_ref[0], preferred_element_type=F32
        )
        odd = jnp.dot(
            jnp.concatenate(odd, axis=0).astype(BF16), back_ref[1], preferred_element_type=F32
        )
        real_cos = even[:pairs] + minus[0][:, :1] * sign
        imag_cos = even[pairs:] + minus[1][:, :1] * sign
        real_sin, imag_sin = odd[:pairs], odd[pairs:]
        own_imag = imag_cos + real_sin
        other_imag = real_sin - imag_cos
        if freq == 0:
            other_imag = jnp.where(is_first, imag_cos - real_sin, other_imag)
        inverse.append(
            (
                jnp.concatenate(
                    [real_cos - imag_sin, real_cos + imag_sin, own_imag, other_imag], axis=0
                )
                * scale
            ).astype(BF16)
        )

    blocks = 4
    count = devices // blocks
    writes = []
    for block in range(blocks):
        rows = place[block * count * 8 : (block + 1) * count * 8]
        placed = [
            split_rows(jnp.dot(rows, inverse[freq], preferred_element_type=F32), 8) for freq in range(2)
        ]
        placed = jnp.concatenate(placed, axis=1).astype(BF16)
        where = pl.ds(block * count, count)
        for lane in range(LANE_BLOCKS):
            out_ref[where, lane * 16 : (lane + 1) * 16, :] = placed[
                :, :, lane * LANES : (lane + 1) * LANES
            ]
        write = pltpu.make_async_copy(out_ref.at[where], out_hbm.at[where], out_sem.at[block])
        write.start()
        writes.append(write)
    for write in writes:
        write.wait()


def surface_kernel(count_ref, m_ref, table_ref, gather_ref, out_hbm, parts_ref, out_ref, out_sem):
    take_parts(m_ref, rows_of_16, gather_ref[...], parts_ref)
    writes = []
    parts = 2
    for slot in range(SLOTS_HELD):
        keep = (slot < count_ref[0]).astype(F32)
        for part in range(parts):
            rows = pl.ds(part * LENGTH // parts, LENGTH // parts)
            out_ref[slot, rows] = (
                jnp.dot(table_ref[rows], parts_ref[slot], preferred_element_type=F32) * keep
            )
            write = pltpu.make_async_copy(
                out_ref.at[slot, rows], out_hbm.at[0, slot, rows], out_sem.at[slot, part]
            )
            write.start()
            writes.append(write)
    for write in writes:
        write.wait()


def per_device(windows, counts, intersection_pairs):
    devices = lax.axis_size(AXES)
    position = lax.axis_index(ORDER).astype(jnp.int32).reshape(1)
    forward, backward, columns, columns_back, gather_slots, gather = packed_tables(devices)
    smem = pl.BlockSpec(memory_space=pltpu.SMEM)
    vmem = pl.BlockSpec(memory_space=pltpu.VMEM)
    hbm = pl.BlockSpec(memory_space=pltpu.HBM)
    in_hbm = lambda x: pltpu.with_memory_space_constraint(x, pltpu.HBM)
    dma = pltpu.SemaphoreType.DMA
    params = pltpu.CompilerParams(vmem_limit_bytes=24 << 20)

    sent = pl.pallas_call(
        forward_kernel,
        in_specs=[hbm, hbm, hbm],
        out_specs=hbm,
        out_shape=pltpu.HBM((devices, TILES, 2, LANES), BF16),
        scratch_shapes=[
            pltpu.SMEM((1, 4), jnp.int32),
            pltpu.VMEM((SLOTS_HELD, LENGTH, LENGTH), BF16),
            pltpu.VMEM((LENGTH, LENGTH), BF16),
            pltpu.VMEM((devices, CHUNK, LANES), BF16),
            pltpu.VMEM((devices, 2, LANES), BF16),
            dma((SLOTS_HELD,)),
            dma((3,)),
            dma((2, 16)),
        ],
        compiler_params=params,
        name="forward_rows",
    )(in_hbm(intersection_pairs), in_hbm(windows[0]), in_hbm(forward))
    moved = lax.all_to_all(sent, ORDER, 0, 0, tiled=True)
    crossed = pl.pallas_call(
        cross_kernel,
        in_specs=[smem, vmem, vmem, vmem, vmem],
        out_specs=hbm,
        out_shape=pltpu.HBM((devices, CHUNK, LANES), BF16),
        scratch_shapes=[
            pltpu.VMEM((devices, CHUNK, LANES), BF16),
            pltpu.VMEM((4, LENGTH, LENGTH), BF16),
            pltpu.VMEM((devices * 2, LANES), F32),
            pltpu.VMEM((devices, CHUNK, LANES), BF16),
            dma((1,)),
            dma((4,)),
        ],
        compiler_params=params,
        name="cross_columns",
    )(position, moved, columns, columns_back, gather_slots)
    returned = lax.all_to_all(crossed, ORDER, 0, 0, tiled=True)
    return pl.pallas_call(
        surface_kernel,
        in_specs=[smem, vmem, vmem, vmem],
        out_specs=hbm,
        out_shape=pltpu.HBM((1, SLOTS_HELD, LENGTH, LENGTH), F32),
        scratch_shapes=[
            pltpu.VMEM((SLOTS_HELD, LENGTH, LENGTH), BF16),
            pltpu.VMEM((SLOTS_HELD, LENGTH, LENGTH), F32),
            dma((4, 2)),
        ],
        compiler_params=params,
        name="surfaces",
    )(counts, returned, backward, gather)


def solution(mesh):
    in_specs = (P(AXES, None, None, None), P(AXES), P(AXES, None))
    out_specs = P(AXES, None, None, None)
    split = Mesh(mesh.devices.reshape(SIZES), AXES)
    return jax.shard_map(
        per_device, mesh=split, in_specs=in_specs, out_specs=out_specs, check_vma=False
    )
```

```python
import jax
import jax.numpy as jnp
import numpy as np
from jax import lax
from jax.experimental import pallas as pl
from jax.experimental.pallas import tpu as pltpu
from jax.sharding import Mesh
from jax.sharding import PartitionSpec as P

AXES = ("x", "y", "core", "z")
SIZES = (4, 4, 2, 4)
ORDER = ("core", "z", "y", "x")
LENGTH = 512
HALF = LENGTH // 2
SLOTS_HELD = 4
LANES = 128
LANE_BLOCKS = LENGTH // LANES
CHUNK = LANE_BLOCKS * 16
TILES = CHUNK // 2 + 1
BF16 = jnp.bfloat16
F32 = jnp.float32


def packed_tables(devices):
    places = np.arange(LENGTH)
    packed = LENGTH // devices
    forward = np.zeros((devices, packed, LENGTH))
    backward = np.zeros((devices, packed, LENGTH))
    for dev in range(devices):
        for part in range(packed):
            freq = dev * (packed // 2) + part // 2
            angle = 2.0 * np.pi * ((freq * places) % LENGTH) / LENGTH
            if part % 2 == 0:
                forward[dev, part] = np.cos(angle)
                backward[dev, part] = np.cos(angle) * (1.0 if freq == 0 else 2.0)
            elif freq == 0:
                forward[dev, part] = 1.0 - 2.0 * (places % 2)
                backward[dev, part] = 1.0 - 2.0 * (places % 2)
            else:
                forward[dev, part] = -np.sin(angle)
                backward[dev, part] = -2.0 * np.sin(angle)
    forward = forward.reshape(2, devices // 2, packed, LENGTH).transpose(1, 0, 2, 3)
    forward = forward.reshape(LENGTH, LENGTH)
    backward = backward.reshape(LENGTH, LENGTH).T / LENGTH
    product = places[:, None] * places[None, :] % LENGTH
    cosine = np.cos(2.0 * np.pi * product / LENGTH)
    sine = np.sin(2.0 * np.pi * product / LENGTH)
    packed_sine = np.concatenate([cosine[:, HALF : HALF + 1], sine[:, 1:HALF]], axis=1)
    columns = np.concatenate([cosine[:, :HALF], packed_sine], axis=1)
    columns_back = np.stack([cosine[:HALF], sine[:HALF]])
    columns_back[1, 0] = 0.0
    order = np.arange(4 * 64)
    gather = np.zeros((4 * 64, 4 * 64))
    gather[order, order % 64 * 4 + order // 64] = 1.0
    dev, slot, part = order % 64 // 4, order % 4, order // 64
    gather_slots = np.zeros((4 * 64, 4 * 64))
    gather_slots[order, slot // 2 * 128 + dev * 8 + slot % 2 * 4 + part] = 1.0
    tables = (forward, backward, columns, columns_back, gather_slots, gather)
    return tuple(jnp.asarray(table.astype(jnp.bfloat16)) for table in tables)


def split_rows(value, rows):
    return value.reshape(value.shape[0] // rows, rows, value.shape[1])


def wide(value):
    return jnp.concatenate([value] * LANE_BLOCKS, axis=1)


def total(value):
    return jnp.sum(jnp.sum(value, axis=0, keepdims=True), axis=1, keepdims=True)


def moments(x_ref, slot):
    rows = 16
    steps = LENGTH // rows
    entries = float(LENGTH * LENGTH)
    base = x_ref[slot, 0:rows, :].astype(F32)
    first = jnp.zeros_like(base)
    second = jnp.zeros_like(base)
    for step in range(1, steps):
        diff = x_ref[slot, step * rows : (step + 1) * rows, :].astype(F32) - base
        first = first + diff
        second = second + diff * diff
    local = base + first * (1.0 / steps)
    mean = total(local) * (steps / entries)
    off = local - mean
    spread = total(second - first * first * (1.0 / steps) + off * off * float(steps))
    return mean, lax.rsqrt(spread * (1.0 / entries) + 1e-05)


def exchange_place(scene):
    z, core, y, x = scene & 3, (scene >> 2) & 1, (scene >> 3) & 3, scene >> 5
    return ((core * 4 + z) * 4 + y) * 4 + x


def forward_kernel(
    pair_hbm,
    x_hbm,
    table_hbm,
    out_hbm,
    pair_ref,
    x_ref,
    table_ref,
    out_ref,
    names_ref,
    in_sem,
    late_sem,
    out_sem,
):
    devices = out_ref.shape[0]
    groups = devices // 2
    blocks = 8
    out_rows = out_hbm.reshape(devices, 2 * TILES, LANES)
    reads = [pltpu.make_async_copy(x_hbm.at[s], x_ref.at[s], in_sem.at[s]) for s in range(SLOTS_HELD)]
    table_read = pltpu.make_async_copy(table_hbm, table_ref, late_sem.at[0])
    pair_read = pltpu.make_async_copy(pair_hbm, pair_ref, late_sem.at[1])
    reads[0].start()
    table_read.start()
    for read in reads[1:]:
        read.start()
    pair_read.start()
    ones = jnp.ones((LENGTH, LANES), BF16)
    spectra = []
    writes = []
    for s in range(SLOTS_HELD):
        if s % 2 == 0:
            continue
        for t in (s - 1, s):
            reads[t].wait()
        if s == 1:
            table_read.wait()
            row_sum = jnp.dot(table_ref[...], ones, preferred_element_type=F32)
        for t in (s - 1, s):
            mean, scale = moments(x_ref, t)
            product = jnp.dot(table_ref[...], x_ref[t], preferred_element_type=F32)
            spectra.append(split_rows(product * scale - wide(row_sum * (mean * scale)), 8))
        if s == 1:
            pair_read.wait()
            column = lax.broadcasted_iota(jnp.int32, (2, LANES), 1) // (LANES // 4)
            named = jnp.zeros((2, LANES), F32)
            for k in range(4):
                value = pair_ref[0, k] if k % 2 else exchange_place(pair_ref[0, k])
                named = jnp.where(column == k, value.astype(F32), named)
            names_ref[...] = jnp.broadcast_to(named[None], (devices, 2, LANES)).astype(BF16)
            write = pltpu.make_async_copy(names_ref, out_hbm.at[:, TILES - 1], late_sem.at[2])
            write.start()
            writes.append(write)
        count = groups // blocks
        for block in range(blocks):
            one, two = (part[block * count : (block + 1) * count] for part in spectra[s - 1 :])
            upper = lax.broadcasted_iota(jnp.int32, one.shape, 1) < 4
            low = jnp.where(upper, one, pltpu.roll(two, 4, 1)).astype(BF16)
            high = jnp.where(upper, pltpu.roll(one, 4, 1), two).astype(BF16)
            for side, filled in enumerate((low, high)):
                place = pl.ds(side * groups + block * count, count)
                for lane in range(LANE_BLOCKS):
                    start = s // 2 * 32 + lane * 8
                    out_ref[place, start : start + 8] = filled[:, :, lane * LANES : (lane + 1) * LANES]
                rows = pl.ds(s // 2 * 32, 32)
                write = pltpu.make_async_copy(
                    out_ref.at[place, rows], out_rows.at[place, rows], out_sem.at[s // 2, 2 * block + side]
                )
                write.start()
                writes.append(write)
    for write in writes:
        write.wait()


def rows_of_16(m_ref, block):
    return jnp.concatenate(
        [
            m_ref[block * 16 : (block + 1) * 16, lane * 16 : (lane + 1) * 16, :].reshape(256, LANES)
            for lane in range(LANE_BLOCKS)
        ],
        axis=1,
    )


def rows_of_8(rows_ref, block):
    tile = lambda k: rows_ref[block * 16 : (block + 1) * 16, k * 8 : (k + 1) * 8].reshape(128, LANES)
    return jnp.concatenate(
        [
            jnp.concatenate([tile(lane), tile(LANE_BLOCKS + lane)], axis=0)
            for lane in range(LANE_BLOCKS)
        ],
        axis=1,
    )


def take_parts(m_ref, rows_of, gather, parts_ref):
    for block in range(m_ref.shape[0] // 16):
        rows = rows_of(m_ref, block)
        taken = jnp.dot(gather, rows, preferred_element_type=F32).astype(BF16)
        for part in range(4):
            parts_ref[part, block * 64 : (block + 1) * 64, :] = taken[part * 64 : (part + 1) * 64]


def cross(real, imag):
    pairs = real.shape[0] // 2
    own_real, other_real = real[:pairs], real[pairs:]
    own_imag, other_imag = imag[:pairs], imag[pairs:]
    return (
        own_real * other_real + own_imag * other_imag,
        own_imag * other_real - own_real * other_imag,
    )


def cross_kernel(
    first_ref, m_ref, columns_ref, back_ref, gather_ref, out_hbm, rows_ref, parts_ref, names_ref,
    out_ref, in_sem, out_sem
):
    devices = m_ref.shape[0]
    slots = devices * SLOTS_HELD
    pairs = devices
    is_first = first_ref[0] == 0

    copy = pltpu.make_async_copy(
        m_ref.reshape(devices, 2 * TILES, LANES).at[:, 0:CHUNK], rows_ref, in_sem.at[0]
    )
    copy.start()
    names_ref[...] = m_ref[:, TILES - 1].astype(F32).reshape(devices * 2, LANES)
    names = names_ref[pl.ds(0, devices, stride=2), :]
    named = [
        jnp.broadcast_to(names[:, k * LANES // 4 : k * LANES // 4 + 1], (devices, LANES))
        for k in range(4)
    ]
    slot_rows = [
        (named[2 * side] * SLOTS_HELD + named[2 * side + 1]).astype(jnp.int32) for side in range(2)
    ]
    same = lax.broadcasted_iota(jnp.int32, (pairs, LANES), 0) == lax.broadcasted_iota(
        jnp.int32, (pairs, LANES), 1
    )
    slot_lanes = [
        jnp.sum(jnp.where(same, slot_rows[side], 0), axis=0, keepdims=True) for side in range(2)
    ]
    wanted = jnp.concatenate([wide(slot_rows[side]) for side in range(2)], axis=0)
    pick = (wanted == lax.broadcasted_iota(jnp.int32, (2 * pairs, slots), 1)).astype(F32).astype(BF16)
    group = lax.broadcasted_iota(jnp.int32, (devices, 8, LANES), 0)
    inner = lax.broadcasted_iota(jnp.int32, (devices, 8, LANES), 1)
    row_code = (group * SLOTS_HELD + ((inner & 3) + (inner >> 2) * slots)).reshape(devices * 8, LANES)
    place = jnp.concatenate(
        [
            (row_code == slot_lanes[side] + part * slots).astype(F32).astype(BF16)
            for part in range(2)
            for side in range(2)
        ],
        axis=1,
    )
    copy.wait()
    take_parts(rows_ref, rows_of_8, gather_ref[...], parts_ref)

    zero = lax.broadcasted_iota(jnp.int32, (2 * pairs, HALF), 1) == 0
    zero_pairs = lax.broadcasted_iota(jnp.int32, (pairs, HALF), 1) == 0
    sign = (1 - 2 * (lax.broadcasted_iota(jnp.int32, (pairs, LENGTH), 1) & 1)).astype(F32)
    scale = 1.0 / (LENGTH * LENGTH)
    picked = [
        jnp.dot(pick, parts_ref[part], preferred_element_type=F32).astype(BF16) for part in range(4)
    ]
    spectra = jnp.dot(
        jnp.concatenate(picked, axis=0), columns_ref[...], preferred_element_type=F32
    )
    inverse = []
    for freq in range(2):
        products = [
            spectra[part * 2 * pairs : (part + 1) * 2 * pairs] for part in (2 * freq, 2 * freq + 1)
        ]
        re_cos, re_sin = products[0][:, :HALF], products[0][:, HALF:]
        im_cos, im_sin = products[1][:, :HALF], products[1][:, HALF:]
        re_odd = jnp.where(zero, 0.0, re_sin)
        im_odd = jnp.where(zero, 0.0, im_sin)
        plus = cross(re_cos + im_odd, im_cos - re_odd)
        minus = cross(
            jnp.where(zero, re_sin, re_cos - im_sin), jnp.where(zero, im_sin, im_cos + re_sin)
        )
        if freq == 0:
            low_plus = cross(re_cos, -re_odd)
            low_minus = cross(jnp.where(zero, re_sin, re_cos), re_odd)
            top_plus = cross(im_cos, -im_odd)
            top_minus = cross(jnp.where(zero, im_sin, im_cos), im_odd)
            plus = (
                jnp.where(is_first, low_plus[0] - top_plus[1], plus[0]),
                jnp.where(is_first, low_plus[1] + top_plus[0], plus[1]),
            )
            minus = (
                jnp.where(is_first, low_minus[0] - top_minus[1], minus[0]),
                jnp.where(is_first, low_minus[1] + top_minus[0], minus[1]),
            )
        even = [jnp.where(zero_pairs, plus[k], plus[k] + minus[k]) for k in range(2)]
        odd = [plus[k] - minus[k] for k in range(2)]
        even = jnp.dot(
            jnp.concatenate(even, axis=0).astype(BF16), back_ref[0], preferred_element_type=F32
        )
        odd = jnp.dot(
            jnp.concatenate(odd, axis=0).astype(BF16), back_ref[1], preferred_element_type=F32
        )
        real_cos = even[:pairs] + minus[0][:, :1] * sign
        imag_cos = even[pairs:] + minus[1][:, :1] * sign
        real_sin, imag_sin = odd[:pairs], odd[pairs:]
        own_imag = imag_cos + real_sin
        other_imag = real_sin - imag_cos
        if freq == 0:
            other_imag = jnp.where(is_first, imag_cos - real_sin, other_imag)
        inverse.append(
            (
                jnp.concatenate(
                    [real_cos - imag_sin, real_cos + imag_sin, own_imag, other_imag], axis=0
                )
                * scale
            ).astype(BF16)
        )

    blocks = 4
    count = devices // blocks
    writes = []
    for block in range(blocks):
        rows = place[block * count * 8 : (block + 1) * count * 8]
        placed = [
            split_rows(jnp.dot(rows, inverse[freq], preferred_element_type=F32), 8) for freq in range(2)
        ]
        placed = jnp.concatenate(placed, axis=1).astype(BF16)
        where = pl.ds(block * count, count)
        for lane in range(LANE_BLOCKS):
            out_ref[where, lane * 16 : (lane + 1) * 16, :] = placed[
                :, :, lane * LANES : (lane + 1) * LANES
            ]
        write = pltpu.make_async_copy(out_ref.at[where], out_hbm.at[where], out_sem.at[block])
        write.start()
        writes.append(write)
    for write in writes:
        write.wait()


def surface_kernel(count_ref, m_ref, table_ref, gather_ref, out_hbm, parts_ref, out_ref, out_sem):
    take_parts(m_ref, rows_of_16, gather_ref[...], parts_ref)
    writes = []
    parts = 2
    for slot in range(SLOTS_HELD):
        keep = (slot < count_ref[0]).astype(F32)
        for part in range(parts):
            rows = pl.ds(part * LENGTH // parts, LENGTH // parts)
            out_ref[slot, rows] = (
                jnp.dot(table_ref[rows], parts_ref[slot], preferred_element_type=F32) * keep
            )
            write = pltpu.make_async_copy(
                out_ref.at[slot, rows], out_hbm.at[0, slot, rows], out_sem.at[slot, part]
            )
            write.start()
            writes.append(write)
    for write in writes:
        write.wait()


def per_device(windows, counts, intersection_pairs):
    devices = lax.axis_size(AXES)
    position = lax.axis_index(ORDER).astype(jnp.int32).reshape(1)
    forward, backward, columns, columns_back, gather_slots, gather = packed_tables(devices)
    smem = pl.BlockSpec(memory_space=pltpu.SMEM)
    vmem = pl.BlockSpec(memory_space=pltpu.VMEM)
    hbm = pl.BlockSpec(memory_space=pltpu.HBM)
    in_hbm = lambda x: pltpu.with_memory_space_constraint(x, pltpu.HBM)
    dma = pltpu.SemaphoreType.DMA
    params = pltpu.CompilerParams(vmem_limit_bytes=24 << 20)

    sent = pl.pallas_call(
        forward_kernel,
        in_specs=[hbm, hbm, hbm],
        out_specs=hbm,
        out_shape=pltpu.HBM((devices, TILES, 2, LANES), BF16),
        scratch_shapes=[
            pltpu.SMEM((1, 4), jnp.int32),
            pltpu.VMEM((SLOTS_HELD, LENGTH, LENGTH), BF16),
            pltpu.VMEM((LENGTH, LENGTH), BF16),
            pltpu.VMEM((devices, CHUNK, LANES), BF16),
            pltpu.VMEM((devices, 2, LANES), BF16),
            dma((SLOTS_HELD,)),
            dma((3,)),
            dma((2, 16)),
        ],
        compiler_params=params,
        name="forward_rows",
    )(in_hbm(intersection_pairs), in_hbm(windows[0]), in_hbm(forward))
    moved = lax.all_to_all(sent, ORDER, 0, 0, tiled=True)
    crossed = pl.pallas_call(
        cross_kernel,
        in_specs=[smem, vmem, vmem, vmem, vmem],
        out_specs=hbm,
        out_shape=pltpu.HBM((devices, CHUNK, LANES), BF16),
        scratch_shapes=[
            pltpu.VMEM((devices, CHUNK, LANES), BF16),
            pltpu.VMEM((4, LENGTH, LENGTH), BF16),
            pltpu.VMEM((devices * 2, LANES), F32),
            pltpu.VMEM((devices, CHUNK, LANES), BF16),
            dma((1,)),
            dma((4,)),
        ],
        compiler_params=params,
        name="cross_columns",
    )(position, moved, columns, columns_back, gather_slots)
    returned = lax.all_to_all(crossed, ORDER, 0, 0, tiled=True)
    return pl.pallas_call(
        surface_kernel,
        in_specs=[smem, vmem, vmem, vmem],
        out_specs=hbm,
        out_shape=pltpu.HBM((1, SLOTS_HELD, LENGTH, LENGTH), F32),
        scratch_shapes=[
            pltpu.VMEM((SLOTS_HELD, LENGTH, LENGTH), BF16),
            pltpu.VMEM((SLOTS_HELD, LENGTH, LENGTH), F32),
            dma((4, 2)),
        ],
        compiler_params=params,
        name="surfaces",
    )(counts, returned, backward, gather)


def solution(mesh):
    in_specs = (P(AXES, None, None, None), P(AXES), P(AXES, None))
    out_specs = P(AXES, None, None, None)
    split = Mesh(mesh.devices.reshape(SIZES), AXES)
    return jax.shard_map(
        per_device, mesh=split, in_specs=in_specs, out_specs=out_specs, check_vma=False
    )
```
